256 devices in a mesh: row: 2 (over core), col: 8 (over z), depth: 16 (over y, x).
Axes of the slice: x: 4, y: 4, z: 8, core: 2. Of those that a mesh axis runs over, the one named last changes fastest.
Arguments:
- tokens: bfloat16 [2560, 4096], P(('depth', 'col'), 'row'), may hold values from -6 to 6
- gate_weight: bfloat16 [4096, 14336], P('row', 'col'), may hold values from -0.09375 to 0.09375
- up_weight: bfloat16 [4096, 14336], P('row', 'col'), may hold values from -0.09375 to 0.09375
- down_weight: bfloat16 [14336, 4096], P('col', 'row'), may hold values from -0.046875 to 0.046875
- cotangent: bfloat16 [2560, 4096], P(('depth', 'col'), 'row'), may hold values from -6 to 6
Outputs:
- layer_out: bfloat16 [2560, 4096], P(('depth', 'col'), 'row')
- input_grad: bfloat16 [2560, 4096], P(('depth', 'col'), 'row')
- gate_grad_w: bfloat16 [4096, 14336], P(('row', 'depth'), 'col')
- up_grad_w: bfloat16 [4096, 14336], P(('row', 'depth'), 'col')
- down_grad_w: bfloat16 [14336, 4096], P('col', ('row', 'depth'))
The draws below stay inside these ranges and needn't reach their ends.
All inputs are finite; a program needn't handle non-finite values.
Results may differ from the reference program's by a relative error of at most 0.0049.
Values may be sent and summed in bfloat16 or wider, within the bound.
No kernel may reach another device: no remote copies, remote signals or barrier semaphores. Data moves between devices by JAX's collectives and lax.ppermute only.
A program may use at most 192 MiB of HBM per device.

```python
import jax
import jax.numpy as jnp
from jax import lax

D = 4096
FF = 14336
TOKENS = 2560


def level_of(rng, extent, cuts, least, high):
    loudness, own = 1.0, jax.random.fold_in(rng, 6)
    for dim, shards_of in cuts:
        heights = jnp.exp(jax.random.uniform(jax.random.fold_in(own, dim), (shards_of,), jnp.float32, least / len(cuts), high / len(cuts)))
        loudness = loudness * jnp.repeat(heights, extent[dim] // shards_of).reshape([-1 if axis == dim else 1 for axis in range(len(extent))])
    return loudness


def normal_values(key, dims, scale, most, shards=(), kind=jnp.bfloat16):
    result = scale * jax.random.normal(key, dims, jnp.float32)
    if shards:
        result = result * level_of(key, dims, shards, -0.22, 0.18)
    return jnp.clip(result, -most, most).astype(kind)


def setup_inputs(seed: int = 0) -> dict:
    key_of = jax.random.split(jax.random.key(seed), 6)
    return {
        "tokens": normal_values(key_of[0], (TOKENS, D), 1.0, 6.0, ((0, 128), (1, 2))),
        "gate_weight": normal_values(key_of[1], (D, FF), D ** -0.5, 0.09375, ((0, 2), (1, 8))),
        "up_weight": normal_values(key_of[2], (D, FF), D ** -0.5, 0.09375, ((0, 2), (1, 8))),
        "down_weight": normal_values(key_of[3], (FF, D), FF ** -0.5, 0.046875, ((0, 8), (1, 2))),
        "cotangent": normal_values(key_of[4], (TOKENS, D), 1.0, 6.0, ((0, 128), (1, 2))),
    }


def matmul(left, right):
    return jnp.dot(left, right, preferred_element_type=jnp.float32)

def contract_rows(left, right):
    return lax.dot_general(left, right, (((0,), (0,)), ((), ())), preferred_element_type=jnp.float32)

def contract_cols(left, right):
    return lax.dot_general(left, right, (((1,), (1,)), ((), ())), preferred_element_type=jnp.float32)

def swiglu_grad(hidden_grad, gate_pre, up_pre):
    logistic = jax.nn.sigmoid(gate_pre)
    gate_grad = (hidden_grad * up_pre * logistic * (1.0 + gate_pre * (1.0 - logistic))).astype(jnp.bfloat16)
    up_grad = (hidden_grad * gate_pre * logistic).astype(jnp.bfloat16)
    return (gate_grad, up_grad)

def reference(tokens, gate_weight, up_weight, down_weight, cotangent):
    gate_pre = matmul(tokens, gate_weight)
    up_pre = matmul(tokens, up_weight)
    hidden = (gate_pre * jax.nn.sigmoid(gate_pre) * up_pre).astype(jnp.bfloat16)
    layer_out = matmul(hidden, down_weight).astype(jnp.bfloat16)
    hidden_grad = contract_cols(cotangent, down_weight)
    gate_grad, up_grad = swiglu_grad(hidden_grad, gate_pre, up_pre)
    input_grad = (contract_cols(gate_grad, gate_weight) + contract_cols(up_grad, up_weight)).astype(jnp.bfloat16)
    gate_grad_w = contract_rows(tokens, gate_grad).astype(jnp.bfloat16)
    up_grad_w = contract_rows(tokens, up_grad).astype(jnp.bfloat16)
    down_grad_w = contract_rows(hidden, cotangent).astype(jnp.bfloat16)
    return (layer_out, input_grad, gate_grad_w, up_grad_w, down_grad_w)
```

```python
import jax
import jax.numpy as jnp
from jax import lax
from jax.sharding import PartitionSpec as P

BF = jnp.bfloat16
F32 = jnp.float32
COLS, SIDE, LANES = 8, 4, 128
ALONG_X = [[SIDE * y + x for x in range(SIDE)] for y in range(SIDE)]
ALONG_Y = [[SIDE * y + x for y in range(SIDE)] for x in range(SIDE)]


def matmul(left, right):
    return jnp.dot(left, right, preferred_element_type=F32)


def contract_rows(left, right):
    return lax.dot_general(left, right, (((0,), (0,)), ((), ())), preferred_element_type=F32)


def contract_cols(left, right):
    return lax.dot_general(left, right, (((1,), (1,)), ((), ())), preferred_element_type=F32)


def to_z(value, step):
    return lax.ppermute(value, "col", [(k, (k + step) % COLS) for k in range(COLS)])


def to_core(value):
    return lax.ppermute(value, "row", [(0, 1), (1, 0)])


def swap(value, groups):
    return lax.all_to_all(
        value, "depth", split_axis=0, concat_axis=0, axis_index_groups=groups, tiled=True
    )


def gather_col(value):
    half = value.shape[0] // 2
    before, after = to_z(value, 1), to_z(value, -1)
    before2, after2 = to_z(value, 2), to_z(value, -2)
    before3, after3 = to_z(before2, 1), to_z(after2, -1)
    far = (to_z(before2[:half], 2), to_z(after2[half:], -2))
    blocks = [value, after, after2, after3, None, before3, before2, before]
    tokens = [far[0] if b is None else b[:half] for b in blocks]
    upstream = [far[1] if b is None else b[half:] for b in blocks]
    return jnp.concatenate(tokens, axis=0), jnp.concatenate(upstream, axis=0)


def swiglu_grad(hidden_grad, gate_pre, up_pre):
    logistic = jax.nn.sigmoid(gate_pre)
    gate_grad = hidden_grad * up_pre * logistic * (1.0 + gate_pre * (1.0 - logistic))
    up_grad = hidden_grad * gate_pre * logistic
    return gate_grad.astype(BF), up_grad.astype(BF)


def body(tokens, gate_weight, up_weight, down_weight, cotangent):
    first = lax.axis_index("row") == 0
    rows = tokens.shape[0]
    half = gate_weight.shape[1] // 2

    def mine(value):
        return jnp.where(first, value[:, :half], value[:, half:])

    def other(value):
        return jnp.where(first, value[:, half:], value[:, :half])

    def both(own, theirs, axis=1):
        return jnp.concatenate(
            [jnp.where(first, own, theirs), jnp.where(first, theirs, own)], axis=axis
        )

    features, upstream = gather_col(jnp.concatenate([tokens, cotangent], axis=0))
    group, model = features.shape

    gate_part = matmul(features, gate_weight)
    up_part = matmul(features, up_weight)
    grad_part = contract_cols(upstream, down_weight)
    sent = to_core(
        jnp.concatenate([other(gate_part), other(up_part), other(grad_part)], axis=1)
    )
    gate_pre = mine(gate_part) + sent[:, :half]
    up_pre = mine(up_part) + sent[:, half : 2 * half]
    hidden_grad = mine(grad_part) + sent[:, 2 * half :]
    hidden = (gate_pre * jax.nn.sigmoid(gate_pre) * up_pre).astype(BF)
    gate_grad, up_grad = swiglu_grad(hidden_grad, gate_pre, up_pre)

    cut = half // LANES // 2 * LANES + LANES
    route_a = jnp.concatenate([hidden, gate_grad[:, :cut]], axis=1)
    route_b = jnp.concatenate([gate_grad[:, cut:], up_grad], axis=1)
    wide_a = swap(jnp.broadcast_to(route_a, (SIDE,) + route_a.shape), ALONG_X)
    wide_b = lax.all_gather(route_b, "depth", axis_index_groups=ALONG_Y)
    wide_a = wide_a.reshape(SIDE * group, -1)
    wide_b = wide_b.reshape(SIDE * group, -1)

    def columns(value, axis, groups):
        split = value.reshape(group, SIDE, SIDE, LANES)
        split = jnp.moveaxis(split, axis, 0).reshape(SIDE, group, SIDE * LANES)
        own = swap(split, groups).reshape(SIDE * group, SIDE * LANES)
        return own, to_core(own)

    feature_a = columns(features, 2, ALONG_X)
    upstream_a = columns(upstream, 2, ALONG_X)
    feature_b = columns(features, 1, ALONG_Y)

    def summed(partial, groups):
        blocks = partial.astype(BF).reshape(2, SIDE, LANES, -1)
        moved = swap(jnp.moveaxis(blocks, 1, 0), groups)
        total = jnp.sum(moved.astype(F32), axis=0).astype(BF)
        return total[0], to_core(total[1])

    part_a = jnp.concatenate(
        [
            jnp.concatenate(
                [
                    contract_rows(upstream_a[k], wide_a[:, :half]),
                    contract_rows(feature_a[k], wide_a[:, half:]),
                ],
                axis=1,
            )
            for k in range(2)
        ],
        axis=0,
    )
    part_b = jnp.concatenate([contract_rows(feature_b[k], wide_b) for k in range(2)], axis=0)
    own_a, theirs_a = summed(part_a, ALONG_Y)
    own_b, theirs_b = summed(part_b, ALONG_X)
    rest = half - cut

    def gate_of(a, b):
        return jnp.concatenate([a[:, half:], b[:, :rest]], axis=1)

    gate_grad_w = both(gate_of(own_a, own_b), gate_of(theirs_a, theirs_b))
    up_grad_w = both(own_b[:, rest:], theirs_b[:, rest:])
    down_grad_w = both(own_a[:, :half], theirs_a[:, :half]).T

    theirs = to_core(jnp.concatenate([hidden, gate_grad, up_grad], axis=1))
    hidden_full = both(hidden, theirs[:, :half])
    gate_full = both(gate_grad, theirs[:, half : 2 * half])
    up_full = both(up_grad, theirs[:, 2 * half :])
    out_part = matmul(hidden_full, down_weight)
    in_part = contract_cols(gate_full, gate_weight) + contract_cols(up_full, up_weight)

    turn = (COLS - lax.axis_index("col")) % COLS
    part = jnp.concatenate([out_part.astype(BF), in_part.astype(BF)], axis=1)
    part = part.reshape(COLS, rows, 2 * model)
    part = lax.dynamic_slice_in_dim(jnp.concatenate([part, part], axis=0), turn, COLS, 0)
    moved = lax.all_to_all(part, "col", split_axis=0, concat_axis=0, tiled=True)
    total = jnp.sum(moved.astype(F32), axis=0).astype(BF)
    return (total[:, :model], total[:, model:], gate_grad_w, up_grad_w, down_grad_w)


def solution(mesh):
    in_specs = (
        P(("depth", "col"), "row"),
        P("row", "col"),
        P("row", "col"),
        P("col", "row"),
        P(("depth", "col"), "row"),
    )
    out_specs = (
        P(("depth", "col"), "row"),
        P(("depth", "col"), "row"),
        P(("row", "depth"), "col"),
        P(("row", "depth"), "col"),
        P("col", ("row", "depth")),
    )
    return jax.shard_map(body, mesh=mesh, in_specs=in_specs, out_specs=out_specs, check_vma=False)
```

```python
import functools

import jax
import jax.numpy as jnp
from jax import lax
from jax.experimental import pallas as pl
from jax.experimental.pallas import tpu as pltpu
from jax.sharding import PartitionSpec as P

BF = jnp.bfloat16
F32 = jnp.float32
COLS, SIDE, LANES = 8, 4, 128
ALONG_X = [[SIDE * y + x for x in range(SIDE)] for y in range(SIDE)]
ALONG_Y = [[SIDE * y + x for y in range(SIDE)] for x in range(SIDE)]
MIB = 1 << 20


def dot(left, right, dims):
    return lax.dot_general(left, right, (dims, ((), ())), preferred_element_type=F32)


def to_z(value, step):
    return lax.ppermute(value, "col", [(k, (k + step) % COLS) for k in range(COLS)])


def to_x(value, step):
    pairs = [(k, k // SIDE * SIDE + (k + step) % SIDE) for k in range(SIDE * SIDE)]
    return lax.ppermute(value, "depth", pairs)


def to_y(value, step):
    side = SIDE * SIDE
    return lax.ppermute(value, "depth", [(k, (k + SIDE * step) % side) for k in range(side)])


def to_core(value):
    return lax.ppermute(value, "row", [(0, 1), (1, 0)])


def swap(value, groups):
    return lax.all_to_all(
        value, "depth", split_axis=0, concat_axis=0, axis_index_groups=groups, tiled=True
    )


def shape(*dims, dtype=BF):
    return jax.ShapeDtypeStruct(dims, dtype)


def call(kernel, outs, *args, limit=32, scratch=()):
    return pl.pallas_call(
        kernel,
        out_shape=outs,
        scratch_shapes=list(scratch),
        compiler_params=pltpu.CompilerParams(vmem_limit_bytes=limit * MIB),
    )(*args)


def assemble_kernel(*refs):
    blocks, (feat, upst, send_a, send_b, feat32, upst32) = refs[: COLS + 1], refs[COLS + 1 :]
    rows = blocks[0].shape[0] // 2
    width = feat.shape[1]
    for k in range(COLS):
        if k < COLS // 2:
            block = blocks[k][...].astype(F32)
        elif k == COLS // 2:
            block = jnp.concatenate([blocks[k][...], blocks[k + 1][...]], axis=1).astype(F32)
        else:
            block = blocks[k + 1][...].astype(F32)
        feat32[pl.ds(rows * k, rows), :] = block[:rows]
        upst32[pl.ds(rows * k, rows), :] = block[rows:]
    feat[...] = feat32[...].astype(BF)
    upst[...] = upst32[...].astype(BF)
    quarter = width // SIDE
    for i in range(SIDE):
        send_b[i] = feat[:, quarter * i : quarter * (i + 1)]
        for j in range(SIDE):
            column = LANES * (SIDE * j + i)
            send_a[i, :, LANES * j : LANES * (j + 1)] = feat[:, column : column + LANES]
            send_a[i, :, quarter + LANES * j : quarter + LANES * (j + 1)] = upst[
                :, column : column + LANES
            ]


def gather_col(value):
    half = value.shape[1] // 2
    before, after = to_z(value, 1), to_z(value, -1)
    before2, after2 = to_z(value, 2), to_z(value, -2)
    before3, after3 = to_z(before2, 1), to_z(after2, -1)
    far = (to_z(before2[:, :half], 2), to_z(after2[:, half:], -2))
    return [value, after, after2, after3, *far, before3, before2, before]


def project_kernel(which, feat, upst, gate, up, down, out):
    width = gate.shape[1]
    products = (
        dot(feat[...], gate[...], ((1,), (0,))),
        dot(feat[...], up[...], ((1,), (0,))),
        dot(upst[...], down[...], ((1,), (1,))),
    )
    for k, product in enumerate(products):
        place = (slice(None), slice(width * k, width * (k + 1)))

        @pl.when(pl.program_id(0) == 0)
        def _():
            out[place] = product

        @pl.when(pl.program_id(0) != 0)
        def _():
            out[place] = out[place] + product


def project(which, features, upstream, gate_weight, up_weight, down_weight):
    group, model = features.shape
    half = gate_weight.shape[1] // 2
    step = model // 4
    return pl.pallas_call(
        project_kernel,
        grid_spec=pltpu.PrefetchScalarGridSpec(
            num_scalar_prefetch=1,
            grid=(model // step,),
            in_specs=[
                pl.BlockSpec((group, step), lambda k, w: (0, k)),
                pl.BlockSpec((group, step), lambda k, w: (0, k)),
                pl.BlockSpec((step, half), lambda k, w: (k, w[0])),
                pl.BlockSpec((step, half), lambda k, w: (k, w[0])),
                pl.BlockSpec((half, step), lambda k, w: (w[0], k)),
            ],
            out_specs=pl.BlockSpec((group, 3 * half), lambda k, w: (0, 0)),
        ),
        out_shape=shape(group, 3 * half, dtype=F32),
        compiler_params=pltpu.CompilerParams(vmem_limit_bytes=24 * MIB),
    )(which, features, upstream, gate_weight, up_weight, down_weight)


def swiglu_kernel(own, theirs, route_a, route_b):
    half = own.shape[1] // 3
    cut = route_a.shape[1] - half
    parts = [slice(half * k, half * (k + 1)) for k in range(3)]
    gate_pre = own[:, parts[0]] + theirs[:, parts[0]]
    up_pre = own[:, parts[1]] + theirs[:, parts[1]]
    hidden_grad = own[:, parts[2]] + theirs[:, parts[2]]
    logistic = jax.nn.sigmoid(gate_pre)
    route_a[:, :half] = (gate_pre * logistic * up_pre).astype(BF)
    gate_grad = hidden_grad * up_pre * logistic * (1.0 + gate_pre * (1.0 - logistic))
    gate_grad = gate_grad.astype(BF)
    route_a[:, half:] = gate_grad[:, :cut]
    route_b[:, : half - cut] = gate_grad[:, cut:]
    route_b[:, half - cut :] = (hidden_grad * gate_pre * logistic).astype(BF)


def back_kernel(place, a_own, b_own, a_theirs, b_theirs, down, gate, up, out, inp, total):
    half = down.shape[0]
    cut = a_own.shape[1] - half
    rest = half - cut
    rows = out.shape[1]
    inner = pl.program_id(1)

    def add(a, b):
        grads = jnp.concatenate([a[:, half:], b[:, :rest]], axis=1)
        first = dot(a[:, :half], down[...], ((1,), (0,)))
        second = dot(grads, gate[...], ((1,), (1,))) + dot(b[:, rest:], up[...], ((1,), (1,)))
        return first, second

    @pl.when(inner == 0)
    def _():
        total[0], total[1] = add(a_own, b_own)

    @pl.when(inner == 1)
    def _():
        first, second = add(a_theirs, b_theirs)
        first = total[0] + first
        second = total[1] + second
        for k in range(COLS):
            at = lax.rem(place[1] + k, COLS)
            out[at] = first[rows * k : rows * (k + 1)].astype(BF)
            inp[at] = second[rows * k : rows * (k + 1)].astype(BF)


def back(place, routes, down_weight, gate_weight, up_weight, rows):
    units, model = down_weight.shape
    half = units // 2
    step = model // 4

    def whole(value):
        return pl.BlockSpec(value.shape, lambda n, j, p: (0, 0))

    def pick(j, p):
        return lax.rem(p[0] + j, 2)

    block = pl.BlockSpec((COLS, rows, step), lambda n, j, p: (0, 0, n))
    return pl.pallas_call(
        back_kernel,
        grid_spec=pltpu.PrefetchScalarGridSpec(
            num_scalar_prefetch=1,
            grid=(model // step, 2),
            in_specs=[whole(r) for r in routes]
            + [
                pl.BlockSpec((half, step), lambda n, j, p: (pick(j, p), n)),
                pl.BlockSpec((step, half), lambda n, j, p: (n, pick(j, p))),
                pl.BlockSpec((step, half), lambda n, j, p: (n, pick(j, p))),
            ],
            out_specs=[block, block],
            scratch_shapes=[pltpu.VMEM((2, COLS * rows, step), F32)],
        ),
        out_shape=[shape(COLS, rows, model)] * 2,
        compiler_params=pltpu.CompilerParams(vmem_limit_bytes=24 * MIB),
    )(place, *routes, down_weight, gate_weight, up_weight)


def weight_kernel(cut, place, *refs):
    pieces, columns = refs[:4], refs[4:6]
    own, before, after, far_a, far_b, total = refs[6:]
    width = SIDE * LANES
    for t in range(2):
        for s, (piece, offset) in enumerate(zip(pieces, (0, SIDE - 1, 1, 2))):
            rows = columns[t][lax.rem(place[0] + offset, SIDE)]
            part = dot(rows[:, :width], piece[:, cut:], ((0,), (0,)))
            total[:, cut:] = part if s == 0 else total[:, cut:] + part
            if cut:
                part = dot(rows[:, width:], piece[:, :cut], ((0,), (0,)))
                total[:, :cut] = part if s == 0 else total[:, :cut] + part
        here = pl.ds(LANES * t, LANES)
        for ref, offset in ((own, 0), (before, SIDE - 1), (after, 1), ((far_a, far_b)[t], 2)):
            start = pl.multiple_of(LANES * lax.rem(place[1] + offset, SIDE), LANES)
            value = total[pl.ds(start, LANES), :]
            if ref is far_a or ref is far_b:
                ref[...] = value.astype(BF)
            else:
                ref[here, :] = value


def weight_partials(cut, place, pieces, columns):
    wide = pieces[0].shape[1]
    vmem = pl.BlockSpec(memory_space=pltpu.VMEM)
    return pl.pallas_call(
        functools.partial(weight_kernel, cut),
        in_specs=[pl.BlockSpec(memory_space=pltpu.SMEM)] + [vmem] * 6,
        out_specs=[vmem] * 5,
        out_shape=[shape(2 * LANES, wide, dtype=F32)] * 3 + [shape(LANES, wide)] * 2,
        scratch_shapes=[pltpu.VMEM((SIDE * LANES, wide), F32)],
        compiler_params=pltpu.CompilerParams(vmem_limit_bytes=32 * MIB),
    )(place, *pieces, *columns)


def pass_on_kernel(before, after, from_before, from_after, send_before, send_after):
    first, second = pl.ds(0, LANES), pl.ds(LANES, LANES)
    send_after[first, :] = (after[first, :] + from_before[...].astype(F32)).astype(BF)
    send_after[second, :] = after[second, :].astype(BF)
    send_before[first, :] = before[first, :].astype(BF)
    send_before[second, :] = (before[second, :] + from_after[...].astype(F32)).astype(BF)


def sum_kernel(own, from_before, from_after, mine, theirs):
    total = own[...] + from_before[...].astype(F32) + from_after[...].astype(F32)
    mine[...] = total[:LANES].astype(BF)
    theirs[...] = total[LANES:].astype(BF)


def scatter(parts, send):
    own, before, after, far_a, far_b = parts
    wide = own.shape[1]
    from_before, from_after = send(far_a, 1), send(far_b, -1)
    pair = [shape(2 * LANES, wide)] * 2
    send_before, send_after = call(pass_on_kernel, pair, before, after, from_before, from_after)
    from_before, from_after = send(send_after, 1), send(send_before, -1)
    pair = [shape(LANES, wide)] * 2
    return call(sum_kernel, pair, own, from_before, from_after)


def gather(value, send):
    before, after = send(value, 1), send(value, -1)
    return [value, before, after, send(before, 1)]


def body(tokens, gate_weight, up_weight, down_weight, cotangent):
    row, col, depth = (lax.axis_index(name) for name in ("row", "col", "depth"))
    first = row == 0
    at_x, at_y = depth % SIDE, depth // SIDE
    rows, model = tokens.shape
    group = rows * COLS
    half = gate_weight.shape[1] // 2
    cut = (half // LANES // 2 + 1) * LANES
    width = SIDE * LANES

    blocks = gather_col(jnp.concatenate([tokens, cotangent], axis=0))
    features, upstream, send_a, send_b = call(
        assemble_kernel,
        [
            shape(group, model),
            shape(group, model),
            shape(SIDE, group, 2 * width),
            shape(SIDE, group, width),
        ],
        *blocks,
        scratch=[pltpu.VMEM((group, model), F32)] * 2,
    )
    weights = (gate_weight, up_weight, down_weight)
    sent = project(jnp.reshape(1 - row, (1,)), features, upstream, *weights)
    kept = project(jnp.reshape(row, (1,)), features, upstream, *weights)
    routes = call(
        swiglu_kernel,
        [shape(group, half + cut), shape(group, 2 * half - cut)],
        kept,
        to_core(sent),
    )
    route_a, route_b = routes

    columns_a = swap(send_a, ALONG_X)
    columns_b = swap(send_b, ALONG_Y)
    columns_a = (columns_a, to_core(columns_a))
    columns_b = (columns_b, to_core(columns_b))

    wide_a = gather(route_a, to_x)
    wide_b = gather(route_b, to_y)

    theirs = (to_core(route_a), to_core(route_b))
    out_part, in_part = back(
        jnp.stack([row, col]),
        (route_a, route_b, *theirs),
        down_weight,
        gate_weight,
        up_weight,
        rows,
    )

    part_a = weight_partials(half, jnp.stack([at_x, at_y]), wide_a, columns_a)
    part_b = weight_partials(0, jnp.stack([at_y, at_x]), wide_b, columns_b)
    mine_a, other_a = scatter(part_a, to_y)
    mine_b, other_b = scatter(part_b, to_x)
    other_a, other_b = to_core(other_a), to_core(other_b)
    rest = half - cut

    def both(own, theirs):
        return jnp.concatenate(
            [jnp.where(first, own, theirs), jnp.where(first, theirs, own)], axis=1
        )

    def gate_of(a, b):
        return jnp.concatenate([a[:, half:], b[:, :rest]], axis=1)

    gate_grad_w = both(gate_of(mine_a, mine_b), gate_of(other_a, other_b))
    up_grad_w = both(mine_b[:, rest:], other_b[:, rest:])
    down_grad_w = both(mine_a[:, :half], other_a[:, :half]).T

    part = jnp.concatenate([out_part, in_part], axis=2)
    moved = lax.all_to_all(part, "col", split_axis=0, concat_axis=0, tiled=True)
    total = jnp.sum(moved.astype(F32), axis=0).astype(BF)
    return (total[:, :model], total[:, model:], gate_grad_w, up_grad_w, down_grad_w)


def solution(mesh):
    in_specs = (
        P(("depth", "col"), "row"),
        P("row", "col"),
        P("row", "col"),
        P("col", "row"),
        P(("depth", "col"), "row"),
    )
    out_specs = (
        P(("depth", "col"), "row"),
        P(("depth", "col"), "row"),
        P(("row", "depth"), "col"),
        P(("row", "depth"), "col"),
        P("col", ("row", "depth")),
    )
    return jax.shard_map(body, mesh=mesh, in_specs=in_specs, out_specs=out_specs, check_vma=False)
```

```python
import functools

import jax
import jax.numpy as jnp
from jax import lax
from jax.experimental import pallas as pl
from jax.experimental.pallas import tpu as pltpu
from jax.sharding import PartitionSpec as P

BF = jnp.bfloat16
F32 = jnp.float32
COLS, SIDE, LANES = 8, 4, 128
ALONG_X = [[SIDE * y + x for x in range(SIDE)] for y in range(SIDE)]
ALONG_Y = [[SIDE * y + x for y in range(SIDE)] for x in range(SIDE)]
MIB = 1 << 20


def dot(left, right, dims):
    return lax.dot_general(left, right, (dims, ((), ())), preferred_element_type=F32)


def to_z(value, step):
    return lax.ppermute(value, "col", [(k, (k + step) % COLS) for k in range(COLS)])


def to_x(value, step):
    pairs = [(k, k // SIDE * SIDE + (k + step) % SIDE) for k in range(SIDE * SIDE)]
    return lax.ppermute(value, "depth", pairs)


def to_y(value, step):
    side = SIDE * SIDE
    return lax.ppermute(value, "depth", [(k, (k + SIDE * step) % side) for k in range(side)])


def to_core(value):
    return lax.ppermute(value, "row", [(0, 1), (1, 0)])


def swap(value, groups):
    return lax.all_to_all(
        value, "depth", split_axis=0, concat_axis=0, axis_index_groups=groups, tiled=True
    )


def shape(*dims, dtype=BF):
    return jax.ShapeDtypeStruct(dims, dtype)


def hbm(*values):
    return [pltpu.with_memory_space_constraint(value, pltpu.HBM) for value in values]


def cost(flops, moved):
    return pl.CostEstimate(flops=flops, bytes_accessed=moved, transcendentals=0)


def call(kernel, outs, *args, limit=16, scratch=()):
    return pl.pallas_call(
        kernel,
        out_shape=outs,
        scratch_shapes=list(scratch),
        compiler_params=pltpu.CompilerParams(vmem_limit_bytes=limit * MIB),
    )(*args)


def assemble_kernel(*refs):
    blocks, (feat, upst, send_a, send_b, feat32, upst32) = refs[: COLS + 1], refs[COLS + 1 :]
    rows = blocks[0].shape[0] // 2
    width = feat.shape[1]
    for k in range(COLS):
        if k < COLS // 2:
            block = blocks[k][...].astype(F32)
        elif k == COLS // 2:
            block = jnp.concatenate([blocks[k][...], blocks[k + 1][...]], axis=1).astype(F32)
        else:
            block = blocks[k + 1][...].astype(F32)
        feat32[pl.ds(rows * k, rows), :] = block[:rows]
        upst32[pl.ds(rows * k, rows), :] = block[rows:]
    feat[...] = feat32[...].astype(BF)
    upst[...] = upst32[...].astype(BF)
    quarter = width // SIDE
    for i in range(SIDE):
        send_b[i] = feat[:, quarter * i : quarter * (i + 1)]
        for j in range(SIDE):
            column = LANES * (SIDE * j + i)
            send_a[i, :, LANES * j : LANES * (j + 1)] = feat[:, column : column + LANES]
            send_a[i, :, quarter + LANES * j : quarter + LANES * (j + 1)] = upst[
                :, column : column + LANES
            ]


def gather_col(value):
    half = value.shape[1] // 2
    before, after = to_z(value, 1), to_z(value, -1)
    before2, after2 = to_z(value, 2), to_z(value, -2)
    before3, after3 = to_z(before2, 1), to_z(after2, -1)
    far = (to_z(before2[:, :half], 2), to_z(after2[:, half:], -2))
    return [value, after, after2, after3, *far, before3, before2, before]


def chunks(extent, size=256):
    return [(start, min(size, extent - start)) for start in range(0, extent, size)]


def project_kernel(which, feat, upst, gate, up, down, out):
    width = gate.shape[1]
    products = (
        dot(feat[...], gate[...], ((1,), (0,))),
        dot(feat[...], up[...], ((1,), (0,))),
        dot(upst[...], down[...], ((1,), (1,))),
    )
    for k, product in enumerate(products):
        place = (slice(None), slice(width * k, width * (k + 1)))

        @pl.when(pl.program_id(0) == 0)
        def _():
            out[place] = product

        @pl.when(pl.program_id(0) != 0)
        def _():
            out[place] = out[place] + product


def project(which, features, upstream, weights):
    group, model = features.shape
    half = weights[0].shape[1] // 2
    step = model // 4
    return pl.pallas_call(
        project_kernel,
        grid_spec=pltpu.PrefetchScalarGridSpec(
            num_scalar_prefetch=1,
            grid=(model // step,),
            in_specs=[
                pl.BlockSpec((group, step), lambda k, w: (0, k)),
                pl.BlockSpec((group, step), lambda k, w: (0, k)),
                pl.BlockSpec((step, half), lambda k, w: (k, w[0])),
                pl.BlockSpec((step, half), lambda k, w: (k, w[0])),
                pl.BlockSpec((half, step), lambda k, w: (w[0], k)),
            ],
            out_specs=pl.BlockSpec((group, 3 * half), lambda k, w: (0, 0)),
        ),
        out_shape=shape(group, 3 * half, dtype=F32),
        cost_estimate=cost(6 * group * model * half, 6 * model * half),
        compiler_params=pltpu.CompilerParams(vmem_limit_bytes=20 * MIB),
    )(which, features, upstream, *hbm(*weights))


def swiglu_kernel(own, theirs, route_a, route_b):
    half = own.shape[1] // 3
    cut = route_a.shape[1] - half
    parts = [slice(half * k, half * (k + 1)) for k in range(3)]
    gate_pre = own[:, parts[0]] + theirs[:, parts[0]]
    up_pre = own[:, parts[1]] + theirs[:, parts[1]]
    hidden_grad = own[:, parts[2]] + theirs[:, parts[2]]
    logistic = jax.nn.sigmoid(gate_pre)
    route_a[:, :half] = (gate_pre * logistic * up_pre).astype(BF)
    gate_grad = hidden_grad * up_pre * logistic * (1.0 + gate_pre * (1.0 - logistic))
    gate_grad = gate_grad.astype(BF)
    route_a[:, half:] = gate_grad[:, :cut]
    route_b[:, : half - cut] = gate_grad[:, cut:]
    route_b[:, half - cut :] = (hidden_grad * gate_pre * logistic).astype(BF)


def back_kernel(place, a_own, b_own, a_theirs, b_theirs, gate, up, down, out, inp, total):
    half = down.shape[0]
    cut = a_own.shape[1] - half
    rest = half - cut
    rows = out.shape[1]
    inner = pl.program_id(1)

    def add(a, b):
        first = dot(a[:, :half], down[...], ((1,), (0,)))
        grads = jnp.concatenate([a[:, half:], b[:, :rest]], axis=1)
        second = dot(grads, gate[...], ((1,), (1,))) + dot(b[:, rest:], up[...], ((1,), (1,)))
        return first, second

    @pl.when(inner == 0)
    def _():
        total[0], total[1] = add(a_own, b_own)

    @pl.when(inner == 1)
    def _():
        first, second = add(a_theirs, b_theirs)
        first = total[0] + first
        second = total[1] + second
        for k in range(COLS):
            at = lax.rem(place[1] + k, COLS)
            block = slice(rows * k, rows * (k + 1))
            out[at] = first[block].astype(BF)
            inp[at] = second[block].astype(BF)


def back(place, routes, weights, rows):
    model, units = weights[0].shape
    half = units // 2
    step = model // 4

    def whole(value):
        return pl.BlockSpec(value.shape, lambda n, j, p: (0, 0))

    def pick(j, p):
        return lax.rem(p[0] + j, 2)

    block = pl.BlockSpec((COLS, rows, step), lambda n, j, p: (0, 0, n))
    return pl.pallas_call(
        back_kernel,
        grid_spec=pltpu.PrefetchScalarGridSpec(
            num_scalar_prefetch=1,
            grid=(model // step, 2),
            in_specs=[whole(r) for r in routes]
            + [
                pl.BlockSpec((step, half), lambda n, j, p: (n, pick(j, p))),
                pl.BlockSpec((step, half), lambda n, j, p: (n, pick(j, p))),
                pl.BlockSpec((half, step), lambda n, j, p: (pick(j, p), n)),
            ],
            out_specs=[block, block],
            scratch_shapes=[pltpu.VMEM((2, COLS * rows, step), F32)],
        ),
        out_shape=[shape(COLS, rows, model)] * 2,
        cost_estimate=cost(6 * COLS * rows * model * units, 6 * model * units),
        compiler_params=pltpu.CompilerParams(vmem_limit_bytes=20 * MIB),
    )(place, *hbm(*routes, *weights))


def weight_kernel(cut, far, place, *refs):
    pieces, columns = refs[:4], refs[4:6]
    outs, (piece, rows, sems) = refs[6:-3], refs[-3:]
    group, wide = pieces[0].shape
    width = SIDE * LANES
    offsets = (2,) if far else (SIDE - 1, 1, 0)
    bases = (0, width) if cut else (0,)
    starts = [lax.rem(place[1] + offset, SIDE) for offset in offsets]
    copies = []
    for s, offset in enumerate((0, SIDE - 1, 1, 2)):
        here = pl.ds(group * s, group)
        source = lax.rem(place[0] + offset, SIDE)
        moves = [(pieces[s], piece.at[here])]
        for t in range(2):
            for i, start in enumerate(starts):
                for j, base in enumerate(bases):
                    at = pl.ds(pl.multiple_of(base + LANES * start, LANES), LANES)
                    to = pl.ds(LANES * (2 * (i * len(bases) + j) + t), LANES)
                    moves.append((columns[t].at[source, :, at], rows.at[here, to]))
        for k, (left, right) in enumerate(moves):
            copies.append(pltpu.make_async_copy(left, right, sems.at[s, k]))
    for copy in copies:
        copy.start()
    for copy in copies:
        copy.wait()
    for i in range(len(offsets)):
        for j, (first, last) in enumerate(((cut, wide), (0, cut))[: len(bases)]):
            column = 2 * LANES * (i * len(bases) + j)
            left = rows[:, column : column + 2 * LANES]
            value = dot(left, piece[:, first:last], ((0,), (0,)))
            if far:
                outs[0][:, first:last] = value[:LANES].astype(BF)
                outs[1][:, first:last] = value[LANES:].astype(BF)
            else:
                outs[i][:, first:last] = value


def weight_partials(cut, far, place, pieces, columns):
    group, wide = pieces[0].shape
    count = (1 if far else 3) * (2 if cut else 1)
    outs = [shape(LANES, wide)] * 2 if far else [shape(2 * LANES, wide, dtype=F32)] * 3
    return pl.pallas_call(
        functools.partial(weight_kernel, cut, far),
        in_specs=[pl.BlockSpec(memory_space=pltpu.SMEM)]
        + [pl.BlockSpec(memory_space=pl.ANY)] * 6,
        out_specs=[pl.BlockSpec(memory_space=pltpu.VMEM)] * len(outs),
        out_shape=outs,
        scratch_shapes=[
            pltpu.VMEM((SIDE * group, wide), BF),
            pltpu.VMEM((SIDE * group, 2 * LANES * count), BF),
            pltpu.SemaphoreType.DMA((SIDE, 1 + 2 * count)),
        ],
        cost_estimate=cost(
            16 * group * LANES * wide * len(outs), 2 * SIDE * group * (wide + 2 * LANES * count)
        ),
        compiler_params=pltpu.CompilerParams(vmem_limit_bytes=20 * MIB),
    )(place, *hbm(*pieces, *columns))


def pass_on_kernel(before, after, from_before, from_after, send_before, send_after):
    first, second = pl.ds(0, LANES), pl.ds(LANES, LANES)
    send_after[first, :] = (after[first, :] + from_before[...].astype(F32)).astype(BF)
    send_after[second, :] = after[second, :].astype(BF)
    send_before[first, :] = before[first, :].astype(BF)
    send_before[second, :] = (before[second, :] + from_after[...].astype(F32)).astype(BF)


def sum_kernel(own, from_before, from_after, mine, theirs):
    total = own[...] + from_before[...].astype(F32) + from_after[...].astype(F32)
    mine[...] = total[:LANES].astype(BF)
    theirs[...] = total[LANES:].astype(BF)


def scatter(cut, place, pieces, columns, send):
    wide = pieces[0].shape[1]
    far_a, far_b = weight_partials(cut, True, place, pieces, columns)
    from_before, from_after = send(far_a, 1), send(far_b, -1)
    before, after, own = weight_partials(cut, False, place, pieces, columns)
    pair = [shape(2 * LANES, wide)] * 2
    send_before, send_after = call(pass_on_kernel, pair, before, after, from_before, from_after)
    from_before, from_after = send(send_after, 1), send(send_before, -1)
    pair = [shape(LANES, wide)] * 2
    return call(sum_kernel, pair, own, from_before, from_after)


def finish_kernel(which, mine_a, other_a, mine_b, other_b, gate, up, down):
    half = gate.shape[1] // 2
    cut = mine_a.shape[1] - half
    rest = half - cut

    def place(a, b, base):
        gate[:, base : base + cut] = a[:, half:]
        gate[:, base + cut : base + half] = b[:, :rest]
        up[:, base : base + half] = b[:, rest:]
        down[base : base + half, :] = a[:, :half].T

    @pl.when(which[0] == 0)
    def _():
        place(mine_a, mine_b, 0)
        place(other_a, other_b, half)

    @pl.when(which[0] != 0)
    def _():
        place(other_a, other_b, 0)
        place(mine_a, mine_b, half)


def total_kernel(moved, out, grad):
    model = out.shape[1]
    total = moved[0].astype(F32)
    for k in range(1, COLS):
        total = total + moved[k].astype(F32)
    out[...] = total[:, :model].astype(BF)
    grad[...] = total[:, model:].astype(BF)


def gather(value, send):
    before, after = send(value, 1), send(value, -1)
    return [value, before, after, send(after, -1)]


def call_at(kernel, outs, which, *args):
    return pl.pallas_call(
        kernel,
        in_specs=[pl.BlockSpec(memory_space=pltpu.SMEM)]
        + [pl.BlockSpec(memory_space=pltpu.VMEM)] * len(args),
        out_shape=outs,
        compiler_params=pltpu.CompilerParams(vmem_limit_bytes=16 * MIB),
    )(which, *args)


def gather(value, send):
    before, after = send(value, 1), send(value, -1)
    return [value, before, after, send(before, 1)]


def body(tokens, gate_weight, up_weight, down_weight, cotangent):
    row, col, depth = (lax.axis_index(name) for name in ("row", "col", "depth"))
    at_x, at_y = depth % SIDE, depth // SIDE
    rows, model = tokens.shape
    group = rows * COLS
    half = gate_weight.shape[1] // 2
    cut = (half // LANES // 2 + 1) * LANES
    width = SIDE * LANES

    blocks = gather_col(jnp.concatenate([tokens, cotangent], axis=0))
    features, upstream, send_a, send_b = call(
        assemble_kernel,
        [
            shape(group, model),
            shape(group, model),
            pltpu.HBM((SIDE, group, 2 * width), BF),
            pltpu.HBM((SIDE, group, width), BF),
        ],
        *blocks,
        scratch=[pltpu.VMEM((group, model), F32)] * 2,
    )
    weights = (gate_weight, up_weight, down_weight)
    sent = project(jnp.reshape(1 - row, (1,)), features, upstream, weights)
    kept = project(jnp.reshape(row, (1,)), features, upstream, weights)
    routes = call(
        swiglu_kernel,
        [pltpu.HBM((group, half + cut), BF), pltpu.HBM((group, 2 * half - cut), BF)],
        kept,
        *hbm(to_core(sent)),
    )
    route_a, route_b = routes
    wide_a = gather(route_a, to_x)
    wide_b = gather(route_b, to_y)

    send_a, _ = lax.optimization_barrier((send_a, sent))
    columns_a = swap(send_a, ALONG_X)
    send_b, _ = lax.optimization_barrier((send_b, wide_a[1]))
    columns_b = swap(send_b, ALONG_Y)
    columns_a = (columns_a, to_core(columns_a))
    columns_b = (columns_b, to_core(columns_b))

    theirs = (to_core(route_a), to_core(route_b))
    routes, _ = lax.optimization_barrier(
        ((route_a, route_b, *theirs), (*wide_a[1:3], *wide_b[1:3]))
    )
    part = back(jnp.stack([row, col]), routes, weights, rows)
    wide_a[1], wide_b[1], part = lax.optimization_barrier((wide_a[1], wide_b[1], part))
    part = jnp.concatenate(part, axis=2)
    moved = lax.all_to_all(part, "col", split_axis=0, concat_axis=0, tiled=True)
    layer_out, input_grad = call(total_kernel, [shape(rows, model)] * 2, moved)

    mine_a, other_a = scatter(half, jnp.stack([at_x, at_y]), wide_a, columns_a, to_y)
    mine_b, other_b = scatter(0, jnp.stack([at_y, at_x]), wide_b, columns_b, to_x)
    weight_grads = call_at(
        finish_kernel,
        [shape(LANES, 2 * half)] * 2 + [shape(2 * half, LANES)],
        jnp.reshape(row, (1,)),
        mine_a,
        to_core(other_a),
        mine_b,
        to_core(other_b),
    )
    return (layer_out, input_grad, *weight_grads)


def solution(mesh):
    in_specs = (
        P(("depth", "col"), "row"),
        P("row", "col"),
        P("row", "col"),
        P("col", "row"),
        P(("depth", "col"), "row"),
    )
    out_specs = (
        P(("depth", "col"), "row"),
        P(("depth", "col"), "row"),
        P(("row", "depth"), "col"),
        P(("row", "depth"), "col"),
        P("col", ("row", "depth")),
    )
    return jax.shard_map(body, mesh=mesh, in_specs=in_specs, out_specs=out_specs, check_vma=False)
```

```python
import functools

import jax
import jax.numpy as jnp
from jax import lax
from jax.experimental import pallas as pl
from jax.experimental.pallas import tpu as pltpu
from jax.sharding import PartitionSpec as P

BF = jnp.bfloat16
F32 = jnp.float32
COLS, SIDE, LANES = 8, 4, 128
ALONG_X = [[SIDE * y + x for x in range(SIDE)] for y in range(SIDE)]
ALONG_Y = [[SIDE * y + x for y in range(SIDE)] for x in range(SIDE)]
MIB = 1 << 20
PROJECT_STEPS, BACK_STEPS = 8, 4


def dot(left, right, dims):
    return lax.dot_general(left, right, (dims, ((), ())), preferred_element_type=F32)


def to_z(value, step):
    return lax.ppermute(value, "col", [(k, (k + step) % COLS) for k in range(COLS)])


def to_x(value, step):
    pairs = [(k, k // SIDE * SIDE + (k + step) % SIDE) for k in range(SIDE * SIDE)]
    return lax.ppermute(value, "depth", pairs)


def to_y(value, step):
    side = SIDE * SIDE
    return lax.ppermute(value, "depth", [(k, (k + SIDE * step) % side) for k in range(side)])


def to_core(value):
    return lax.ppermute(value, "row", [(0, 1), (1, 0)])


def swap(value, groups):
    return lax.all_to_all(
        value, "depth", split_axis=0, concat_axis=0, axis_index_groups=groups, tiled=True
    )


def shape(*dims, dtype=BF):
    return jax.ShapeDtypeStruct(dims, dtype)


def hbm(*values):
    return [pltpu.with_memory_space_constraint(value, pltpu.HBM) for value in values]


def cost(flops, moved):
    return pl.CostEstimate(flops=flops, bytes_accessed=moved, transcendentals=0)


def call(kernel, outs, *args, limit=16, scratch=()):
    return pl.pallas_call(
        kernel,
        out_shape=outs,
        scratch_shapes=list(scratch),
        compiler_params=pltpu.CompilerParams(vmem_limit_bytes=limit * MIB),
    )(*args)


def assemble_kernel(*refs):
    blocks, (feat, upst, send_a, send_b, feat32, upst32) = refs[: COLS + 1], refs[COLS + 1 :]
    rows = blocks[0].shape[0] // 2
    width = feat.shape[1]
    for k in range(COLS):
        if k < COLS // 2:
            block = blocks[k][...].astype(F32)
        elif k == COLS // 2:
            block = jnp.concatenate([blocks[k][...], blocks[k + 1][...]], axis=1).astype(F32)
        else:
            block = blocks[k + 1][...].astype(F32)
        feat32[pl.ds(rows * k, rows), :] = block[:rows]
        upst32[pl.ds(rows * k, rows), :] = block[rows:]
    feat[...] = feat32[...].astype(BF)
    upst[...] = upst32[...].astype(BF)
    quarter = width // SIDE
    for i in range(SIDE):
        send_b[i] = feat[:, quarter * i : quarter * (i + 1)]
        for j in range(SIDE):
            column = LANES * (SIDE * j + i)
            send_a[i, :, LANES * j : LANES * (j + 1)] = feat[:, column : column + LANES]
            send_a[i, :, quarter + LANES * j : quarter + LANES * (j + 1)] = upst[
                :, column : column + LANES
            ]


def gather_col(value):
    half = value.shape[1] // 2
    before, after = to_z(value, 1), to_z(value, -1)
    before2, after2 = to_z(value, 2), to_z(value, -2)
    before3, after3 = to_z(before2, 1), to_z(after2, -1)
    far = (to_z(before2[:, :half], 2), to_z(after2[:, half:], -2))
    return [value, after, after2, after3, *far, before3, before2, before]


def chunks(extent, size=256):
    return [(start, min(size, extent - start)) for start in range(0, extent, size)]


def project_kernel(which, feat, upst, gate, up, down, out):
    width = gate.shape[1]
    products = (
        dot(feat[...], gate[...], ((1,), (0,))),
        dot(feat[...], up[...], ((1,), (0,))),
        dot(upst[...], down[...], ((1,), (1,))),
    )
    for k, product in enumerate(products):
        place = (slice(None), slice(width * k, width * (k + 1)))

        @pl.when(pl.program_id(0) == 0)
        def _():
            out[place] = product

        @pl.when(pl.program_id(0) != 0)
        def _():
            out[place] = out[place] + product


def project(which, features, upstream, weights):
    group, model = features.shape
    half = weights[0].shape[1] // 2
    step = model // PROJECT_STEPS
    return pl.pallas_call(
        project_kernel,
        grid_spec=pltpu.PrefetchScalarGridSpec(
            num_scalar_prefetch=1,
            grid=(model // step,),
            in_specs=[
                pl.BlockSpec((group, step), lambda k, w: (0, k)),
                pl.BlockSpec((group, step), lambda k, w: (0, k)),
                pl.BlockSpec((step, half), lambda k, w: (k, w[0])),
                pl.BlockSpec((step, half), lambda k, w: (k, w[0])),
                pl.BlockSpec((half, step), lambda k, w: (w[0], k)),
            ],
            out_specs=pl.BlockSpec((group, 3 * half), lambda k, w: (0, 0)),
        ),
        out_shape=shape(group, 3 * half, dtype=F32),
        cost_estimate=cost(6 * group * model * half, 6 * model * half),
        compiler_params=pltpu.CompilerParams(vmem_limit_bytes=20 * MIB),
    )(which, features, upstream, *hbm(*weights))


def swiglu_kernel(own, theirs, route_a, route_b, grads):
    half = own.shape[1] // 3
    cut = route_a.shape[1] - half
    parts = [slice(half * k, half * (k + 1)) for k in range(3)]
    gate_pre = own[:, parts[0]] + theirs[:, parts[0]]
    up_pre = own[:, parts[1]] + theirs[:, parts[1]]
    hidden_grad = own[:, parts[2]] + theirs[:, parts[2]]
    logistic = jax.nn.sigmoid(gate_pre)
    hidden = (gate_pre * logistic * up_pre).astype(BF)
    gate_grad = hidden_grad * up_pre * logistic * (1.0 + gate_pre * (1.0 - logistic))
    gate_grad = gate_grad.astype(BF)
    up_grad = (hidden_grad * gate_pre * logistic).astype(BF)
    route_a[:, :half] = hidden
    route_a[:, half:] = gate_grad[:, :cut]
    route_b[:, : half - cut] = gate_grad[:, cut:]
    route_b[:, half - cut :] = up_grad
    for part, value in zip(parts, (gate_grad, up_grad, hidden)):
        grads[:, part] = value


def back_kernel(place, own, theirs, gate, up, down, out, total):
    half = down.shape[0]
    rows, step = out.shape[1], gate.shape[0]
    inner = pl.program_id(1)

    def add(grads):
        first = dot(grads[:, 2 * half :], down[...], ((1,), (0,)))
        second = dot(grads[:, :half], gate[...], ((1,), (1,)))
        second = second + dot(grads[:, half : 2 * half], up[...], ((1,), (1,)))
        return first, second

    @pl.when(inner == 0)
    def _():
        total[:, :step], total[:, step:] = add(own)

    @pl.when(inner == 1)
    def _():
        first, second = add(theirs)
        total[:, :step] = total[:, :step] + first
        total[:, step:] = total[:, step:] + second
        for k in range(COLS):
            at = lax.rem(place[1] + k, COLS)
            out[at] = total[pl.ds(rows * k, rows), :].astype(BF)


def back(place, grads, weights, rows):
    model, units = weights[0].shape
    half = units // 2
    step = model // BACK_STEPS

    def whole(value):
        return pl.BlockSpec(value.shape, lambda n, j, p: (0, 0))

    def pick(j, p):
        return lax.rem(p[0] + j, 2)

    return pl.pallas_call(
        back_kernel,
        grid_spec=pltpu.PrefetchScalarGridSpec(
            num_scalar_prefetch=1,
            grid=(BACK_STEPS, 2),
            in_specs=[whole(g) for g in grads]
            + [
                pl.BlockSpec((step, half), lambda n, j, p: (n, pick(j, p))),
                pl.BlockSpec((step, half), lambda n, j, p: (n, pick(j, p))),
                pl.BlockSpec((half, step), lambda n, j, p: (pick(j, p), n)),
            ],
            out_specs=pl.BlockSpec((COLS, rows, 2 * step), lambda n, j, p: (0, 0, n)),
            scratch_shapes=[pltpu.VMEM((COLS * rows, 2 * step), F32)],
        ),
        out_shape=shape(COLS, rows, 2 * model),
        cost_estimate=cost(6 * COLS * rows * model * units, 6 * model * units),
        compiler_params=pltpu.CompilerParams(vmem_limit_bytes=20 * MIB),
    )(place, *hbm(*grads, *weights))


def weight_kernel(cut, far, place, *refs):
    pieces, columns = refs[:4], refs[4:6]
    outs, (piece, rows, sems) = refs[6:-3], refs[-3:]
    group, wide = pieces[0].shape
    width = SIDE * LANES
    offsets = (2,) if far else (SIDE - 1, 1, 0)
    bases = (0, width) if cut else (0,)
    starts = [lax.rem(place[1] + offset, SIDE) for offset in offsets]
    copies = []
    for s, offset in enumerate((0, SIDE - 1, 1, 2)):
        here = pl.ds(group * s, group)
        source = lax.rem(place[0] + offset, SIDE)
        moves = [(pieces[s], piece.at[here])]
        for t in range(2):
            for i, start in enumerate(starts):
                for j, base in enumerate(bases):
                    at = pl.ds(pl.multiple_of(base + LANES * start, LANES), LANES)
                    to = pl.ds(LANES * (2 * (i * len(bases) + j) + t), LANES)
                    moves.append((columns[t].at[source, :, at], rows.at[here, to]))
        for k, (left, right) in enumerate(moves):
            copies.append(pltpu.make_async_copy(left, right, sems.at[s, k]))
    for copy in copies:
        copy.start()
    for copy in copies:
        copy.wait()
    for i in range(len(offsets)):
        for j, (first, last) in enumerate(((cut, wide), (0, cut))[: len(bases)]):
            column = 2 * LANES * (i * len(bases) + j)
            left = rows[:, column : column + 2 * LANES]
            value = dot(left, piece[:, first:last], ((0,), (0,)))
            if far:
                outs[0][:, first:last] = value[:LANES].astype(BF)
                outs[1][:, first:last] = value[LANES:].astype(BF)
            else:
                outs[i][:, first:last] = value


def weight_partials(cut, far, place, pieces, columns):
    group, wide = pieces[0].shape
    count = (1 if far else 3) * (2 if cut else 1)
    outs = [shape(LANES, wide)] * 2 if far else [shape(2 * LANES, wide, dtype=F32)] * 3
    return pl.pallas_call(
        functools.partial(weight_kernel, cut, far),
        in_specs=[pl.BlockSpec(memory_space=pltpu.SMEM)]
        + [pl.BlockSpec(memory_space=pl.ANY)] * 6,
        out_specs=[pl.BlockSpec(memory_space=pltpu.VMEM)] * len(outs),
        out_shape=outs,
        scratch_shapes=[
            pltpu.VMEM((SIDE * group, wide), BF),
            pltpu.VMEM((SIDE * group, 2 * LANES * count), BF),
            pltpu.SemaphoreType.DMA((SIDE, 1 + 2 * count)),
        ],
        cost_estimate=cost(
            16 * group * LANES * wide * len(outs), 2 * SIDE * group * (wide + 2 * LANES * count)
        ),
        compiler_params=pltpu.CompilerParams(vmem_limit_bytes=20 * MIB),
    )(place, *hbm(*pieces, *columns))


def pass_on_kernel(before, after, from_before, from_after, send_before, send_after):
    first, second = pl.ds(0, LANES), pl.ds(LANES, LANES)
    send_after[first, :] = (after[first, :] + from_before[...].astype(F32)).astype(BF)
    send_after[second, :] = after[second, :].astype(BF)
    send_before[first, :] = before[first, :].astype(BF)
    send_before[second, :] = (before[second, :] + from_after[...].astype(F32)).astype(BF)


def sum_kernel(own, from_before, from_after, mine, theirs):
    total = own[...] + from_before[...].astype(F32) + from_after[...].astype(F32)
    mine[...] = total[:LANES].astype(BF)
    theirs[...] = total[LANES:].astype(BF)


def scatter(cut, place, pieces, columns, send):
    wide = pieces[0].shape[1]
    far_a, far_b = weight_partials(cut, True, place, pieces, columns)
    from_before, from_after = send(far_a, 1), send(far_b, -1)
    before, after, own = weight_partials(cut, False, place, pieces, columns)
    pair = [shape(2 * LANES, wide)] * 2
    send_before, send_after = call(pass_on_kernel, pair, before, after, from_before, from_after)
    from_before, from_after = send(send_after, 1), send(send_before, -1)
    pair = [shape(LANES, wide)] * 2
    return call(sum_kernel, pair, own, from_before, from_after)


def finish_kernel(which, mine_a, other_a, mine_b, other_b, gate, up, down):
    half = gate.shape[1] // 2
    cut = mine_a.shape[1] - half
    rest = half - cut

    def place(a, b, base):
        gate[:, base : base + cut] = a[:, half:]
        gate[:, base + cut : base + half] = b[:, :rest]
        up[:, base : base + half] = b[:, rest:]
        down[base : base + half, :] = a[:, :half].T

    @pl.when(which[0] == 0)
    def _():
        place(mine_a, mine_b, 0)
        place(other_a, other_b, half)

    @pl.when(which[0] != 0)
    def _():
        place(other_a, other_b, 0)
        place(mine_a, mine_b, half)


def total_kernel(moved, out, grad):
    step = out.shape[1] // BACK_STEPS
    total = moved[0].astype(F32)
    for k in range(1, COLS):
        total = total + moved[k].astype(F32)
    total = total.astype(BF)
    for n in range(BACK_STEPS):
        out[:, step * n : step * (n + 1)] = total[:, 2 * step * n : step * (2 * n + 1)]
        grad[:, step * n : step * (n + 1)] = total[:, step * (2 * n + 1) : 2 * step * (n + 1)]


def gather(value, send):
    before, after = send(value, 1), send(value, -1)
    return [value, before, after, send(after, -1)]


def call_at(kernel, outs, which, *args):
    return pl.pallas_call(
        kernel,
        in_specs=[pl.BlockSpec(memory_space=pltpu.SMEM)]
        + [pl.BlockSpec(memory_space=pltpu.VMEM)] * len(args),
        out_shape=outs,
        compiler_params=pltpu.CompilerParams(vmem_limit_bytes=16 * MIB),
    )(which, *args)


def gather(value, send):
    before, after = send(value, 1), send(value, -1)
    return [value, before, after, send(before, 1)]


def body(tokens, gate_weight, up_weight, down_weight, cotangent):
    row, col, depth = (lax.axis_index(name) for name in ("row", "col", "depth"))
    at_x, at_y = depth % SIDE, depth // SIDE
    rows, model = tokens.shape
    group = rows * COLS
    half = gate_weight.shape[1] // 2
    cut = (half // LANES // 2 + 1) * LANES
    width = SIDE * LANES

    blocks = gather_col(jnp.concatenate([tokens, cotangent], axis=0))
    features, upstream, send_a, send_b = call(
        assemble_kernel,
        [
            shape(group, model),
            shape(group, model),
            pltpu.HBM((SIDE, group, 2 * width), BF),
            pltpu.HBM((SIDE, group, width), BF),
        ],
        *blocks,
        scratch=[pltpu.VMEM((group, model), F32)] * 2,
    )
    weights = (gate_weight, up_weight, down_weight)
    sent = project(jnp.reshape(1 - row, (1,)), features, upstream, weights)
    kept = project(jnp.reshape(row, (1,)), features, upstream, weights)
    routes = call(
        swiglu_kernel,
        [pltpu.HBM((group, n), BF) for n in (half + cut, 2 * half - cut, 3 * half)],
        kept,
        *hbm(to_core(sent)),
    )
    route_a, route_b, grads = routes
    wide_a = gather(route_a, to_x)
    wide_b = gather(route_b, to_y)

    send_a, _ = lax.optimization_barrier((send_a, sent))
    columns_a = swap(send_a, ALONG_X)
    send_b, _ = lax.optimization_barrier((send_b, wide_a[1]))
    columns_b = swap(send_b, ALONG_Y)
    columns_a = (columns_a, to_core(columns_a))
    columns_b = (columns_b, to_core(columns_b))

    grads, _ = lax.optimization_barrier(
        ((grads, to_core(grads)), (*wide_a[1:3], *wide_b[1:3]))
    )
    part = back(jnp.stack([row, col]), grads, weights, rows)
    wide_a[1], wide_b[1], part = lax.optimization_barrier((wide_a[1], wide_b[1], part))
    part, _ = lax.optimization_barrier((part, (wide_a[3], wide_b[3])))
    moved = lax.all_to_all(part, "col", split_axis=0, concat_axis=0, tiled=True)
    layer_out, input_grad = call(total_kernel, [shape(rows, model)] * 2, moved)

    mine_a, other_a = scatter(half, jnp.stack([at_x, at_y]), wide_a, columns_a, to_y)
    mine_b, other_b = scatter(0, jnp.stack([at_y, at_x]), wide_b, columns_b, to_x)
    weight_grads = call_at(
        finish_kernel,
        [shape(LANES, 2 * half)] * 2 + [shape(2 * half, LANES)],
        jnp.reshape(row, (1,)),
        mine_a,
        to_core(other_a),
        mine_b,
        to_core(other_b),
    )
    return (layer_out, input_grad, *weight_grads)


def solution(mesh):
    in_specs = (
        P(("depth", "col"), "row"),
        P("row", "col"),
        P("row", "col"),
        P("col", "row"),
        P(("depth", "col"), "row"),
    )
    out_specs = (
        P(("depth", "col"), "row"),
        P(("depth", "col"), "row"),
        P(("row", "depth"), "col"),
        P(("row", "depth"), "col"),
        P("col", ("row", "depth")),
    )
    return jax.shard_map(body, mesh=mesh, in_specs=in_specs, out_specs=out_specs, check_vma=False)
```

```python
import functools

import jax
import jax.numpy as jnp
from jax import lax
from jax.experimental import pallas as pl
from jax.experimental.pallas import tpu as pltpu
from jax.sharding import PartitionSpec as P

BF = jnp.bfloat16
F32 = jnp.float32
COLS, SIDE, LANES = 8, 4, 128
ALONG_X = [[SIDE * y + x for x in range(SIDE)] for y in range(SIDE)]
ALONG_Y = [[SIDE * y + x for y in range(SIDE)] for x in range(SIDE)]
MIB = 1 << 20
CHUNK = 512


def dot(left, right, dims):
    return lax.dot_general(left, right, (dims, ((), ())), preferred_element_type=F32)


def to_z(value, step):
    return lax.ppermute(value, "col", [(k, (k + step) % COLS) for k in range(COLS)])


def to_x(value, step):
    pairs = [(k, k // SIDE * SIDE + (k + step) % SIDE) for k in range(SIDE * SIDE)]
    return lax.ppermute(value, "depth", pairs)


def to_y(value, step):
    side = SIDE * SIDE
    return lax.ppermute(value, "depth", [(k, (k + SIDE * step) % side) for k in range(side)])


def to_core(value):
    return lax.ppermute(value, "row", [(0, 1), (1, 0)])


def swap(value, groups):
    return lax.all_to_all(
        value, "depth", split_axis=0, concat_axis=0, axis_index_groups=groups, tiled=True
    )


def shape(*dims, dtype=BF):
    return jax.ShapeDtypeStruct(dims, dtype)


def hbm(*values):
    return [pltpu.with_memory_space_constraint(value, pltpu.HBM) for value in values]


def cost(flops, moved):
    return pl.CostEstimate(flops=flops, bytes_accessed=moved, transcendentals=0)


def call(kernel, outs, *args, limit=16, scratch=()):
    return pl.pallas_call(
        kernel,
        out_shape=outs,
        scratch_shapes=list(scratch),
        compiler_params=pltpu.CompilerParams(vmem_limit_bytes=limit * MIB),
    )(*args)


def assemble(blocks, feat, upst, send_a, send_b, feat32, upst32):
    rows = blocks[0].shape[0] // 2
    width = feat.shape[1]
    for k in range(COLS):
        if k < COLS // 2:
            block = blocks[k][...].astype(F32)
        elif k == COLS // 2:
            block = jnp.concatenate([blocks[k][...], blocks[k + 1][...]], axis=1).astype(F32)
        else:
            block = blocks[k + 1][...].astype(F32)
        feat32[pl.ds(rows * k, rows), :] = block[:rows]
        upst32[pl.ds(rows * k, rows), :] = block[rows:]
    feat[...] = feat32[...].astype(BF)
    upst[...] = upst32[...].astype(BF)
    quarter = width // SIDE
    for i in range(SIDE):
        send_b[i] = feat[:, quarter * i : quarter * (i + 1)]
        for j in range(SIDE):
            column = LANES * (SIDE * j + i)
            send_a[i, :, LANES * j : LANES * (j + 1)] = feat[:, column : column + LANES]
            send_a[i, :, quarter + LANES * j : quarter + LANES * (j + 1)] = upst[
                :, column : column + LANES
            ]


def gather_col(value):
    half = value.shape[1] // 2
    before, after = to_z(value, 1), to_z(value, -1)
    before2, after2 = to_z(value, 2), to_z(value, -2)
    before3, after3 = to_z(before2, 1), to_z(after2, -1)
    far = (to_z(before2[:, :half], 2), to_z(after2[:, half:], -2))
    return [value, after, after2, after3, *far, before3, before2, before]


def chunks(extent):
    return [(start, min(CHUNK, extent - start)) for start in range(0, extent, CHUNK)]


def started(moves, sems):
    copies = [pltpu.make_async_copy(*move, sems.at[k]) for k, move in enumerate(moves)]
    for copy in copies:
        copy.start()
    return copies


def weight_moves(which, weights, targets):
    model, half = targets[0].shape
    own = pl.ds(pl.multiple_of(which[0] * half, LANES), half)
    gate, up, down = weights
    moves = []
    for at in [pl.ds(*c) for c in chunks(model)]:
        moves += [(gate.at[at, own], targets[0].at[at]), (up.at[at, own], targets[1].at[at])]
    return moves + [(down.at[own], targets[2])]


def products(copies, feat, upst, weights, out):
    model, half = weights[0].shape
    for k, (start, size) in enumerate(chunks(model)):
        at = slice(start, start + size)
        for j in range(2):
            copies[2 * k + j].wait()
            product = dot(feat[:, at], weights[j][at, :], ((1,), (0,)))
            place = slice(half * j, half * (j + 1))
            out[:, place] = product if k == 0 else out[:, place] + product
    copies[-1].wait()
    out[:, 2 * half :] = dot(upst[...], weights[2][...], ((1,), (1,)))


def first_kernel(which, *refs):
    blocks, weights, outs = refs[: COLS + 1], refs[COLS + 1 : COLS + 4], refs[COLS + 4 : COLS + 9]
    out, *assembled = outs
    *targets, feat32, upst32, sems = refs[COLS + 9 :]
    copies = started(weight_moves(which, weights, targets), sems)
    assemble(blocks, *assembled, feat32, upst32)
    products(copies, *assembled[:2], targets, out)


def second_kernel(which, feat, upst, gate, up, down, out, *scratch):
    targets, sems = scratch[:3], scratch[3]
    copies = started(weight_moves(which, (gate, up, down), targets), sems)
    products(copies, feat, upst, targets, out)


def in_hbm(kernel, outs, which, vmem, operands, scratch, copies, work, limit):
    return pl.pallas_call(
        kernel,
        in_specs=[pl.BlockSpec(memory_space=pltpu.SMEM)]
        + [pl.BlockSpec(memory_space=pltpu.VMEM)] * len(vmem)
        + [pl.BlockSpec(memory_space=pl.ANY)] * len(operands),
        out_specs=jax.tree.map(
            lambda out: (
                pl.BlockSpec(memory_space=pltpu.VMEM)
                if isinstance(out, jax.ShapeDtypeStruct)
                else pl.BlockSpec()
            ),
            outs,
        ),
        out_shape=outs,
        scratch_shapes=[pltpu.VMEM(*s) for s in scratch] + [pltpu.SemaphoreType.DMA((copies,))],
        cost_estimate=cost(*work),
        compiler_params=pltpu.CompilerParams(vmem_limit_bytes=limit * MIB),
    )(which, *vmem, *hbm(*operands))


def project(which, arrays, weights, rows=None):
    model, units = weights[0].shape
    half = units // 2
    group = COLS * rows if rows else arrays[0].shape[0]
    outs = [shape(group, 3 * half, dtype=F32)]
    scratch = [((model, half), BF)] * 2 + [((half, model), BF)]
    if rows:
        width = SIDE * LANES
        outs += [shape(group, model)] * 2
        outs += [pltpu.HBM((SIDE, group, n), BF) for n in (2 * width, width)]
        scratch += [((group, model), F32)] * 2
    return in_hbm(
        first_kernel if rows else second_kernel,
        outs,
        jnp.reshape(which, (1,)),
        arrays,
        weights,
        scratch,
        2 * len(chunks(model)) + 1,
        (0, 0),
        28,
    )


def swiglu_kernel(own, theirs, route_a, route_b, grads):
    half = own.shape[1] // 3
    cut = route_a.shape[1] - half
    parts = [slice(half * k, half * (k + 1)) for k in range(3)]
    gate_pre = own[:, parts[0]] + theirs[:, parts[0]]
    up_pre = own[:, parts[1]] + theirs[:, parts[1]]
    hidden_grad = own[:, parts[2]] + theirs[:, parts[2]]
    logistic = jax.nn.sigmoid(gate_pre)
    hidden = (gate_pre * logistic * up_pre).astype(BF)
    gate_grad = hidden_grad * up_pre * logistic * (1.0 + gate_pre * (1.0 - logistic))
    gate_grad = gate_grad.astype(BF)
    up_grad = (hidden_grad * gate_pre * logistic).astype(BF)
    route_a[:, :half] = hidden
    route_a[:, half:] = gate_grad[:, :cut]
    route_b[:, : half - cut] = gate_grad[:, cut:]
    route_b[:, half - cut :] = up_grad
    for part, value in zip(parts, (gate_grad, up_grad, hidden)):
        grads[:, part] = value


def whole_moves(place, half, own, theirs, parts, targets):
    moves = []
    for part, target in zip(parts, targets):
        for source, which in ((own, place[0]), (theirs, 1 - place[0])):
            at = pl.ds(pl.multiple_of(which * half, LANES), half)
            moves.append((source.at[:, pl.ds(half * part, half)], target.at[:, at]))
    return moves


def store_blocks(place, out, total, base):
    rows, width = out.shape[1], total.shape[1]
    for k in range(COLS):
        at = lax.rem(place[1] + k, COLS)
        out[at, :, base : base + width] = total[pl.ds(rows * k, rows), :].astype(BF)


def forward_kernel(place, theirs, own, down, out, hidden, down_v, total, sems):
    units = down.shape[0]
    moves = whole_moves(place, units // 2, own, theirs, (2,), (hidden,))
    moves += [(down.at[pl.ds(*c)], down_v.at[pl.ds(*c)]) for c in chunks(units)]
    copies = started(moves, sems)
    copies[0].wait()
    copies[1].wait()
    for k, (start, size) in enumerate(chunks(units)):
        at = slice(start, start + size)
        copies[2 + k].wait()
        product = dot(hidden[:, at], down_v[at, :], ((1,), (0,)))
        total[...] = product if k == 0 else total[...] + product
    store_blocks(place, out, total, 0)


def backward_kernel(
    place, first, theirs, own, gate, up, out, gate_g, up_g, gate_v, up_v, total, sems
):
    model, units = gate.shape
    moves = whole_moves(place, units // 2, own, theirs, (0, 1), (gate_g, up_g))
    for at in [pl.ds(*c) for c in chunks(model)]:
        moves += [(gate.at[at], gate_v.at[at]), (up.at[at], up_v.at[at])]
    moves.append((first, out.at[:, :, pl.ds(0, model)]))
    copies = started(moves, sems)
    for copy in copies[:4]:
        copy.wait()
    for k, (start, size) in enumerate(chunks(model)):
        at = slice(start, start + size)
        copies[4 + 2 * k].wait()
        copies[5 + 2 * k].wait()
        product = dot(gate_g[...], gate_v[at, :], ((1,), (1,)))
        total[:, at] = product + dot(up_g[...], up_v[at, :], ((1,), (1,)))
    store_blocks(place, out, total, model)
    copies[-1].wait()


def forward(place, grads, down_weight, rows):
    units, model = down_weight.shape
    group = COLS * rows
    return in_hbm(
        forward_kernel,
        shape(COLS, rows, model),
        place,
        grads[1:],
        (grads[0], down_weight),
        [((group, units), BF), ((units, model), BF), ((group, model), F32)],
        2 + len(chunks(units)),
        (2 * group * model * units, 2 * model * units),
        16,
    )


def backward(place, grads, gate_weight, up_weight, first, rows):
    model, units = gate_weight.shape
    group = COLS * rows
    return in_hbm(
        backward_kernel,
        shape(COLS, rows, 2 * model),
        place,
        (first, grads[1]),
        (grads[0], gate_weight, up_weight),
        [((group, units), BF)] * 2 + [((model, units), BF)] * 2 + [((group, model), F32)],
        5 + 2 * len(chunks(model)),
        (4 * group * model * units, 4 * model * units),
        28,
    )


def weight_kernel(cut, place, *refs):
    pieces = (*refs[1:4], refs[0])
    own, before, after, far_a, far_b, piece, columns, sems = refs[6:]
    group, wide = pieces[0].shape
    width = SIDE * LANES
    around = (0, SIDE - 1, 1, 2)
    moves = [(pieces[s], piece.at[pl.ds(group * s, group)]) for s in range(SIDE)]
    moves += [(refs[4 + t], columns.at[t]) for t in range(2)]
    sources = [lax.rem(place[0] + offset, SIDE) for offset in around]
    for copy in started(moves, sems):
        copy.wait()
    for ref, offset in ((far_a, 2), (after, 1), (before, SIDE - 1), (own, 0)):
        start = LANES * lax.rem(place[1] + offset, SIDE)
        for first, last, base in ((0, cut, width), (cut, wide, 0)):
            if first == last:
                continue
            at = pl.ds(pl.multiple_of(base + start, LANES), LANES)
            left = jnp.concatenate(
                [
                    jnp.concatenate([columns[t, source, :, at] for t in range(2)], axis=1)
                    for source in sources
                ],
                axis=0,
            )
            value = dot(left, piece[:, first:last], ((0,), (0,)))
            if ref is far_a:
                far_a[:, first:last] = value[:LANES].astype(BF)
                far_b[:, first:last] = value[LANES:].astype(BF)
            else:
                ref[:, first:last] = value.astype(ref.dtype)


def weight_partials(cut, place, pieces, columns):
    group, wide = pieces[0].shape
    tokens, width = SIDE * group, columns[0].shape[2]
    return in_hbm(
        functools.partial(weight_kernel, cut),
        [shape(2 * LANES, wide, dtype=F32)]
        + [shape(2 * LANES, wide)] * 2
        + [shape(LANES, wide)] * 2,
        place,
        pieces[3:],
        (*pieces[:3], *columns),
        [((tokens, wide), BF), ((2, *columns[0].shape), BF)],
        SIDE + 2,
        (16 * tokens * LANES * wide, 2 * tokens * (wide + 2 * width)),
        20,
    )


def pass_on_kernel(before, after, from_before, from_after, send_before, send_after):
    first, second = pl.ds(0, LANES), pl.ds(LANES, LANES)
    total = after[first, :].astype(F32) + from_before[...].astype(F32)
    send_after[first, :] = total.astype(BF)
    send_after[second, :] = after[second, :]
    send_before[first, :] = before[first, :]
    total = before[second, :].astype(F32) + from_after[...].astype(F32)
    send_before[second, :] = total.astype(BF)


def sum_kernel(own, from_before, from_after, mine, theirs):
    total = own[...] + from_before[...].astype(F32) + from_after[...].astype(F32)
    mine[...] = total[:LANES].astype(BF)
    theirs[...] = total[LANES:].astype(BF)


def scatter(cut, place, pieces, columns, send):
    wide = pieces[0].shape[1]
    own, before, after, far_a, far_b = weight_partials(cut, place, pieces, columns)
    from_before, from_after = send(far_a, 1), send(far_b, -1)
    pair = [shape(2 * LANES, wide)] * 2
    send_before, send_after = call(pass_on_kernel, pair, before, after, from_before, from_after)
    return own, send(send_after, 1), send(send_before, -1)


def finish_kernel(which, mine_a, other_a, mine_b, other_b, gate, up, down):
    half = gate.shape[1] // 2
    cut = mine_a.shape[1] - half
    rest = half - cut

    def place(a, b, base):
        gate[:, base : base + cut] = a[:, half:]
        gate[:, base + cut : base + half] = b[:, :rest]
        up[:, base : base + half] = b[:, rest:]
        down[base : base + half, :] = a[:, :half].T

    @pl.when(which[0] == 0)
    def _():
        place(mine_a, mine_b, 0)
        place(other_a, other_b, half)

    @pl.when(which[0] != 0)
    def _():
        place(other_a, other_b, 0)
        place(mine_a, mine_b, half)


def total_kernel(moved, out, grad):
    model = out.shape[1]
    total = moved[0].astype(F32)
    for k in range(1, COLS):
        total = total + moved[k].astype(F32)
    out[...] = total[:, :model].astype(BF)
    grad[...] = total[:, model:].astype(BF)


def call_at(kernel, outs, which, *args):
    return pl.pallas_call(
        kernel,
        in_specs=[pl.BlockSpec(memory_space=pltpu.SMEM)]
        + [pl.BlockSpec(memory_space=pltpu.VMEM)] * len(args),
        out_shape=outs,
        compiler_params=pltpu.CompilerParams(vmem_limit_bytes=16 * MIB),
    )(which, *args)


def gather(value, send):
    before, after = send(value, 1), send(value, -1)
    return [value, before, after, send(before, 1)]


def body(tokens, gate_weight, up_weight, down_weight, cotangent):
    row, col, depth = (lax.axis_index(name) for name in ("row", "col", "depth"))
    at_x, at_y = depth % SIDE, depth // SIDE
    rows, model = tokens.shape
    group = rows * COLS
    half = gate_weight.shape[1] // 2
    cut = (half // LANES // 2 + 1) * LANES

    blocks = gather_col(jnp.concatenate([tokens, cotangent], axis=0))
    weights = (gate_weight, up_weight, down_weight)
    sent, features, upstream, send_a, send_b = project(1 - row, blocks, weights, rows)
    (kept,) = project(row, (features, upstream), weights)
    route_a, route_b, grads = call(
        swiglu_kernel,
        [pltpu.HBM((group, n), BF) for n in (half + cut, 2 * half - cut, 3 * half)],
        kept,
        *hbm(to_core(sent)),
    )
    columns_a = swap(send_a, ALONG_X)

    grads = (grads, to_core(grads))
    before_a, after_a = to_x(route_a, 1), to_x(route_a, -1)
    before_b, after_b = to_y(route_b, 1), to_y(route_b, -1)
    place = jnp.stack([row, col])
    first = forward(place, grads, down_weight, rows)
    columns_a, send_b, first = lax.optimization_barrier((columns_a, send_b, first))
    columns_b = swap(send_b, ALONG_Y)
    columns_a = (columns_a, to_core(columns_a))
    columns_b = (columns_b, to_core(columns_b))

    before_a, after_b, first = lax.optimization_barrier((before_a, after_b, first))
    grads, _ = lax.optimization_barrier((grads, (before_a, before_b, after_a, after_b)))
    part = backward(place, grads, gate_weight, up_weight, first, rows)
    wide_a = [route_a, before_a, after_a, to_x(before_a, 1)]
    wide_b = [route_b, before_b, after_b, to_y(after_b, -1)]
    wide_a[1], wide_b[1], part = lax.optimization_barrier((wide_a[1], wide_b[1], part))
    part, _ = lax.optimization_barrier((part, (wide_a[3], wide_b[3])))
    moved = lax.all_to_all(part, "col", split_axis=0, concat_axis=0, tiled=True)
    layer_out, input_grad = call(total_kernel, [shape(rows, model)] * 2, moved)

    moved_a = scatter(half, jnp.stack([at_x, at_y]), wide_a, columns_a, to_y)
    moved_b = scatter(0, jnp.stack([at_y, at_x]), wide_b, columns_b, to_x)
    pair = [shape(LANES, moved_a[0].shape[1])] * 2
    moved_a, layer_out = lax.optimization_barrier((moved_a, layer_out))
    mine_a, other_a = call(sum_kernel, pair, *moved_a)
    pair = [shape(LANES, moved_b[0].shape[1])] * 2
    mine_b, other_b = call(sum_kernel, pair, *moved_b)
    weight_grads = call_at(
        finish_kernel,
        [shape(LANES, 2 * half)] * 2 + [shape(2 * half, LANES)],
        jnp.reshape(row, (1,)),
        mine_a,
        to_core(other_a),
        mine_b,
        to_core(other_b),
    )
    return (layer_out, input_grad, *weight_grads)


def solution(mesh):
    in_specs = (
        P(("depth", "col"), "row"),
        P("row", "col"),
        P("row", "col"),
        P("col", "row"),
        P(("depth", "col"), "row"),
    )
    out_specs = (
        P(("depth", "col"), "row"),
        P(("depth", "col"), "row"),
        P(("row", "depth"), "col"),
        P(("row", "depth"), "col"),
        P("col", ("row", "depth")),
    )
    return jax.shard_map(body, mesh=mesh, in_specs=in_specs, out_specs=out_specs, check_vma=False)
```

```python
import functools

import jax
import jax.numpy as jnp
from jax import lax
from jax.experimental import pallas as pl
from jax.experimental.pallas import tpu as pltpu
from jax.sharding import PartitionSpec as P

BF = jnp.bfloat16
F32 = jnp.float32
COLS, SIDE, LANES = 8, 4, 128
ALONG_X = [[SIDE * y + x for x in range(SIDE)] for y in range(SIDE)]
ALONG_Y = [[SIDE * y + x for y in range(SIDE)] for x in range(SIDE)]
MIB = 1 << 20
CHUNK = 512


def dot(left, right, dims):
    return lax.dot_general(left, right, (dims, ((), ())), preferred_element_type=F32)


def to_z(value, step):
    return lax.ppermute(value, "col", [(k, (k + step) % COLS) for k in range(COLS)])


def to_x(value, step):
    pairs = [(k, k // SIDE * SIDE + (k + step) % SIDE) for k in range(SIDE * SIDE)]
    return lax.ppermute(value, "depth", pairs)


def to_y(value, step):
    side = SIDE * SIDE
    return lax.ppermute(value, "depth", [(k, (k + SIDE * step) % side) for k in range(side)])


def to_core(value):
    return lax.ppermute(value, "row", [(0, 1), (1, 0)])


def swap(value, groups):
    return lax.all_to_all(
        value, "depth", split_axis=0, concat_axis=0, axis_index_groups=groups, tiled=True
    )


def shape(*dims, dtype=BF):
    return jax.ShapeDtypeStruct(dims, dtype)


def hbm(*values):
    return [pltpu.with_memory_space_constraint(value, pltpu.HBM) for value in values]


def cost(flops, moved):
    return pl.CostEstimate(flops=flops, bytes_accessed=moved, transcendentals=0)


def call(kernel, outs, *args, limit=16, scratch=()):
    return pl.pallas_call(
        kernel,
        out_shape=outs,
        scratch_shapes=list(scratch),
        compiler_params=pltpu.CompilerParams(vmem_limit_bytes=limit * MIB),
    )(*args)


def assemble(blocks, feat, upst, send_a, send_b, feat32, upst32):
    rows = blocks[0].shape[0] // 2
    width = feat.shape[1]
    for k in range(COLS):
        if k < COLS // 2:
            block = blocks[k][...].astype(F32)
        elif k == COLS // 2:
            block = jnp.concatenate([blocks[k][...], blocks[k + 1][...]], axis=1).astype(F32)
        else:
            block = blocks[k + 1][...].astype(F32)
        feat32[pl.ds(rows * k, rows), :] = block[:rows]
        upst32[pl.ds(rows * k, rows), :] = block[rows:]
    feat[...] = feat32[...].astype(BF)
    upst[...] = upst32[...].astype(BF)
    quarter = width // SIDE
    for i in range(SIDE):
        send_b[i] = feat[:, quarter * i : quarter * (i + 1)]
        for j in range(SIDE):
            column = LANES * (SIDE * j + i)
            send_a[i, :, LANES * j : LANES * (j + 1)] = feat[:, column : column + LANES]
            send_a[i, :, quarter + LANES * j : quarter + LANES * (j + 1)] = upst[
                :, column : column + LANES
            ]


def gather_col(value):
    half = value.shape[1] // 2
    before, after = to_z(value, 1), to_z(value, -1)
    before2, after2 = to_z(value, 2), to_z(value, -2)
    before3, after3 = to_z(before2, 1), to_z(after2, -1)
    far = (to_z(before2[:, :half], 2), to_z(after2[:, half:], -2))
    return [value, after, after2, after3, *far, before3, before2, before]


def started(moves, sems):
    copies = [pltpu.make_async_copy(*move, sems.at[k]) for k, move in enumerate(moves)]
    for copy in copies:
        copy.start()
    return copies


def weight_copies(which, weights, targets, sems):
    model, half = targets[0].shape
    own = pl.ds(pl.multiple_of(which[0] * half, LANES), half)

    def pair(k):
        at = pl.ds(pl.multiple_of(CHUNK * k, CHUNK), CHUNK)
        return [
            pltpu.make_async_copy(weights[j].at[at, own], targets[j].at[at], sems.at[2 * k + j])
            for j in range(2)
        ]

    last = pltpu.make_async_copy(weights[2].at[own], targets[2], sems.at[2 * model // CHUNK])
    for k in range(model // CHUNK):
        for copy in pair(k):
            copy.start()
    last.start()
    return pair, last


def products(copies, feat, upst, weights, out):
    model, half = weights[0].shape
    pair, last = copies
    out[:, : 2 * half] = jnp.zeros((out.shape[0], 2 * half), F32)

    def step(k, carry):
        at = pl.ds(pl.multiple_of(CHUNK * k, CHUNK), CHUNK)
        for j, copy in enumerate(pair(k)):
            copy.wait()
            place = slice(half * j, half * (j + 1))
            out[:, place] += dot(feat[:, at], weights[j][at, :], ((1,), (0,)))
        return carry

    lax.fori_loop(0, model // CHUNK, step, 0)
    last.wait()
    out[:, 2 * half :] = dot(upst[...], weights[2][...], ((1,), (1,)))


def first_kernel(which, *refs):
    blocks, weights, outs = refs[: COLS + 1], refs[COLS + 1 : COLS + 4], refs[COLS + 4 : COLS + 9]
    out, *assembled = outs
    *targets, feat32, upst32, sems = refs[COLS + 9 :]
    copies = weight_copies(which, weights, targets, sems)
    assemble(blocks, *assembled, feat32, upst32)
    products(copies, *assembled[:2], targets, out)


def second_kernel(which, feat, upst, gate, up, down, out, *scratch):
    targets, sems = scratch[:3], scratch[3]
    copies = weight_copies(which, (gate, up, down), targets, sems)
    products(copies, feat, upst, targets, out)


def in_hbm(kernel, outs, which, vmem, operands, scratch, copies, work, limit):
    return pl.pallas_call(
        kernel,
        in_specs=[pl.BlockSpec(memory_space=pltpu.SMEM)]
        + [pl.BlockSpec(memory_space=pltpu.VMEM)] * len(vmem)
        + [pl.BlockSpec(memory_space=pl.ANY)] * len(operands),
        out_specs=jax.tree.map(
            lambda out: (
                pl.BlockSpec(memory_space=pltpu.VMEM)
                if isinstance(out, jax.ShapeDtypeStruct)
                else pl.BlockSpec()
            ),
            outs,
        ),
        out_shape=outs,
        scratch_shapes=[pltpu.VMEM(*s) for s in scratch] + [pltpu.SemaphoreType.DMA((copies,))],
        cost_estimate=cost(*work),
        compiler_params=pltpu.CompilerParams(vmem_limit_bytes=limit * MIB),
    )(which, *vmem, *hbm(*operands))


def project(which, arrays, weights, rows=None):
    model, units = weights[0].shape
    half = units // 2
    group = COLS * rows if rows else arrays[0].shape[0]
    outs = [shape(group, 3 * half, dtype=F32)]
    scratch = [((model, half), BF)] * 2 + [((half, model), BF)]
    if rows:
        width = SIDE * LANES
        outs += [shape(group, model)] * 2
        outs += [pltpu.HBM((SIDE, group, n), BF) for n in (2 * width, width)]
        scratch += [((group, model), F32)] * 2
    return in_hbm(
        first_kernel if rows else second_kernel,
        outs,
        jnp.reshape(which, (1,)),
        arrays,
        weights,
        scratch,
        2 * model // CHUNK + 1,
        (0, 0),
        28,
    )


def swiglu_kernel(own, theirs, route_a, route_b, grads):
    half = own.shape[1] // 3
    cut = route_a.shape[1] - half
    parts = [slice(half * k, half * (k + 1)) for k in range(3)]
    gate_pre = own[:, parts[0]] + theirs[:, parts[0]]
    up_pre = own[:, parts[1]] + theirs[:, parts[1]]
    hidden_grad = own[:, parts[2]] + theirs[:, parts[2]]
    logistic = jax.nn.sigmoid(gate_pre)
    hidden = (gate_pre * logistic * up_pre).astype(BF)
    gate_grad = hidden_grad * up_pre * logistic * (1.0 + gate_pre * (1.0 - logistic))
    gate_grad = gate_grad.astype(BF)
    up_grad = (hidden_grad * gate_pre * logistic).astype(BF)
    route_a[:, :half] = hidden
    route_a[:, half:] = gate_grad[:, :cut]
    route_b[:, : half - cut] = gate_grad[:, cut:]
    route_b[:, half - cut :] = up_grad
    for part, value in zip(parts, (gate_grad, up_grad, hidden)):
        grads[:, part] = value


def whole_moves(place, half, own, theirs, parts, targets):
    moves = []
    for part, target in zip(parts, targets):
        for source, which in ((own, place[0]), (theirs, 1 - place[0])):
            at = pl.ds(pl.multiple_of(which * half, LANES), half)
            moves.append((source.at[:, pl.ds(half * part, half)], target.at[:, at]))
    return moves


def store_blocks(place, out, total, base):
    rows, width = out.shape[1], total.shape[1]
    for k in range(COLS):
        at = lax.rem(place[1] + k, COLS)
        out[at, :, base : base + width] = total[pl.ds(rows * k, rows), :].astype(BF)


def forward_kernel(place, theirs, own, down, out, hidden, down_v, total, sems):
    units = down.shape[0]
    size = CHUNK // 2
    moves = whole_moves(place, units // 2, own, theirs, (2,), (hidden,))
    copies = started(moves, sems)

    def part(k):
        at = pl.ds(pl.multiple_of(size * k, size), size)
        return pltpu.make_async_copy(down.at[at], down_v.at[at], sems.at[2 + k])

    for k in range(units // size):
        part(k).start()
    total[...] = jnp.zeros(total.shape, F32)
    for copy in copies:
        copy.wait()

    def step(k, carry):
        part(k).wait()
        at = pl.ds(pl.multiple_of(size * k, size), size)
        total[...] += dot(hidden[:, at], down_v[at, :], ((1,), (0,)))
        return carry

    lax.fori_loop(0, units // size, step, 0)
    store_blocks(place, out, total, 0)


def backward_kernel(
    place, first, theirs, own, gate, up, out, gate_g, up_g, gate_v, up_v, total, sems
):
    model, units = gate.shape
    moves = whole_moves(place, units // 2, own, theirs, (0, 1), (gate_g, up_g))
    moves.append((first, out.at[:, :, pl.ds(0, model)]))
    copies = started(moves, sems)

    def pair(k):
        at = pl.ds(pl.multiple_of(CHUNK * k, CHUNK), CHUNK)
        return [
            pltpu.make_async_copy(source.at[at], target.at[at], sems.at[5 + 2 * k + j])
            for j, (source, target) in enumerate(((gate, gate_v), (up, up_v)))
        ]

    for k in range(model // CHUNK):
        for copy in pair(k):
            copy.start()
    for copy in copies:
        copy.wait()

    def step(k, carry):
        for copy in pair(k):
            copy.wait()
        at = pl.ds(pl.multiple_of(CHUNK * k, CHUNK), CHUNK)
        product = dot(gate_g[...], gate_v[at, :], ((1,), (1,)))
        total[:, at] = product + dot(up_g[...], up_v[at, :], ((1,), (1,)))
        return carry

    lax.fori_loop(0, model // CHUNK, step, 0)
    store_blocks(place, out, total, model)


def forward(place, grads, down_weight, rows):
    units, model = down_weight.shape
    group = COLS * rows
    return in_hbm(
        forward_kernel,
        shape(COLS, rows, model),
        place,
        grads[1:],
        (grads[0], down_weight),
        [((group, units), BF), ((units, model), BF), ((group, model), F32)],
        2 + 2 * units // CHUNK,
        (2 * group * model * units, 2 * model * units),
        16,
    )


def backward(place, grads, gate_weight, up_weight, first, rows):
    model, units = gate_weight.shape
    group = COLS * rows
    return in_hbm(
        backward_kernel,
        shape(COLS, rows, 2 * model),
        place,
        (first, grads[1]),
        (grads[0], gate_weight, up_weight),
        [((group, units), BF)] * 2 + [((model, units), BF)] * 2 + [((group, model), F32)],
        5 + 2 * model // CHUNK,
        (4 * group * model * units, 4 * model * units),
        28,
    )


def weight_kernel(cut, place, *refs):
    pieces = (*refs[1:4], refs[0])
    own, before, after, far_a, far_b, piece, columns, sems = refs[6:]
    group, wide = pieces[0].shape
    width = SIDE * LANES
    around = (0, SIDE - 1, 1, 2)
    moves = [(pieces[s], piece.at[pl.ds(group * s, group)]) for s in range(SIDE)]
    moves += [(refs[4 + t], columns.at[t]) for t in range(2)]
    sources = [lax.rem(place[0] + offset, SIDE) for offset in around]
    for copy in started(moves, sems):
        copy.wait()
    for ref, offset in ((far_a, 2), (after, 1), (before, SIDE - 1), (own, 0)):
        start = LANES * lax.rem(place[1] + offset, SIDE)
        for first, last, base in ((0, cut, width), (cut, wide, 0)):
            if first == last:
                continue
            at = pl.ds(pl.multiple_of(base + start, LANES), LANES)
            left = jnp.concatenate(
                [
                    jnp.concatenate([columns[t, source, :, at] for t in range(2)], axis=1)
                    for source in sources
                ],
                axis=0,
            )
            value = dot(left, piece[:, first:last], ((0,), (0,)))
            if ref is far_a:
                far_a[:, first:last] = value[:LANES].astype(BF)
                far_b[:, first:last] = value[LANES:].astype(BF)
            else:
                ref[:, first:last] = value.astype(ref.dtype)


def weight_partials(cut, place, pieces, columns):
    group, wide = pieces[0].shape
    tokens, width = SIDE * group, columns[0].shape[2]
    return in_hbm(
        functools.partial(weight_kernel, cut),
        [shape(2 * LANES, wide, dtype=F32)]
        + [shape(2 * LANES, wide)] * 2
        + [shape(LANES, wide)] * 2,
        place,
        pieces[3:],
        (*pieces[:3], *columns),
        [((tokens, wide), BF), ((2, *columns[0].shape), BF)],
        SIDE + 2,
        (16 * tokens * LANES * wide, 2 * tokens * (wide + 2 * width)),
        20,
    )


def pass_on_kernel(before, after, from_before, from_after, send_before, send_after):
    first, second = pl.ds(0, LANES), pl.ds(LANES, LANES)
    total = after[first, :].astype(F32) + from_before[...].astype(F32)
    send_after[first, :] = total.astype(BF)
    send_after[second, :] = after[second, :]
    send_before[first, :] = before[first, :]
    total = before[second, :].astype(F32) + from_after[...].astype(F32)
    send_before[second, :] = total.astype(BF)


def sum_kernel(own, from_before, from_after, mine, theirs):
    total = own[...] + from_before[...].astype(F32) + from_after[...].astype(F32)
    mine[...] = total[:LANES].astype(BF)
    theirs[...] = total[LANES:].astype(BF)


def scatter(cut, place, pieces, columns, send):
    wide = pieces[0].shape[1]
    own, before, after, far_a, far_b = weight_partials(cut, place, pieces, columns)
    from_before, from_after = send(far_a, 1), send(far_b, -1)
    pair = [shape(2 * LANES, wide)] * 2
    send_before, send_after = call(pass_on_kernel, pair, before, after, from_before, from_after)
    return own, send(send_after, 1), send(send_before, -1)


def finish_kernel(which, mine_a, other_a, mine_b, other_b, gate, up, down):
    half = gate.shape[1] // 2
    cut = mine_a.shape[1] - half
    rest = half - cut

    def place(a, b, base):
        gate[:, base : base + cut] = a[:, half:]
        gate[:, base + cut : base + half] = b[:, :rest]
        up[:, base : base + half] = b[:, rest:]
        down[base : base + half, :] = a[:, :half].T

    @pl.when(which[0] == 0)
    def _():
        place(mine_a, mine_b, 0)
        place(other_a, other_b, half)

    @pl.when(which[0] != 0)
    def _():
        place(other_a, other_b, 0)
        place(mine_a, mine_b, half)


def total_kernel(moved, out, grad):
    model = out.shape[1]
    total = moved[0].astype(F32)
    for k in range(1, COLS):
        total = total + moved[k].astype(F32)
    out[...] = total[:, :model].astype(BF)
    grad[...] = total[:, model:].astype(BF)


def call_at(kernel, outs, which, *args):
    return pl.pallas_call(
        kernel,
        in_specs=[pl.BlockSpec(memory_space=pltpu.SMEM)]
        + [pl.BlockSpec(memory_space=pltpu.VMEM)] * len(args),
        out_shape=outs,
        compiler_params=pltpu.CompilerParams(vmem_limit_bytes=16 * MIB),
    )(which, *args)


def gather(value, send):
    before, after = send(value, 1), send(value, -1)
    return [value, before, after, send(before, 1)]


def body(tokens, gate_weight, up_weight, down_weight, cotangent):
    row, col, depth = (lax.axis_index(name) for name in ("row", "col", "depth"))
    at_x, at_y = depth % SIDE, depth // SIDE
    rows, model = tokens.shape
    group = rows * COLS
    half = gate_weight.shape[1] // 2
    cut = (half // LANES // 2 + 1) * LANES

    blocks = gather_col(jnp.concatenate([tokens, cotangent], axis=0))
    weights = (gate_weight, up_weight, down_weight)
    sent, features, upstream, send_a, send_b = project(1 - row, blocks, weights, rows)
    (kept,) = project(row, (features, upstream), weights)
    route_a, route_b, grads = call(
        swiglu_kernel,
        [pltpu.HBM((group, n), BF) for n in (half + cut, 2 * half - cut, 3 * half)],
        kept,
        *hbm(to_core(sent)),
    )
    columns_a = swap(send_a, ALONG_X)

    grads = (grads, to_core(grads))
    before_a, after_a = to_x(route_a, 1), to_x(route_a, -1)
    before_b, after_b = to_y(route_b, 1), to_y(route_b, -1)
    place = jnp.stack([row, col])
    first = forward(place, grads, down_weight, rows)
    columns_a, send_b, first = lax.optimization_barrier((columns_a, send_b, first))
    columns_b = swap(send_b, ALONG_Y)
    columns_a = (columns_a, to_core(columns_a))
    columns_b = (columns_b, to_core(columns_b))

    before_a, after_b, first = lax.optimization_barrier((before_a, after_b, first))
    grads, _ = lax.optimization_barrier((grads, (before_a, before_b, after_a, after_b)))
    part = backward(place, grads, gate_weight, up_weight, first, rows)
    wide_a = [route_a, before_a, after_a, to_x(before_a, 1)]
    wide_b = [route_b, before_b, after_b, to_y(after_b, -1)]
    wide_a[1], wide_b[1], part = lax.optimization_barrier((wide_a[1], wide_b[1], part))
    part, _ = lax.optimization_barrier((part, (wide_a[3], wide_b[3])))
    moved = lax.all_to_all(part, "col", split_axis=0, concat_axis=0, tiled=True)
    layer_out, input_grad = call(total_kernel, [shape(rows, model)] * 2, moved)

    moved_a = scatter(half, jnp.stack([at_x, at_y]), wide_a, columns_a, to_y)
    moved_b = scatter(0, jnp.stack([at_y, at_x]), wide_b, columns_b, to_x)
    pair = [shape(LANES, moved_a[0].shape[1])] * 2
    moved_a, layer_out = lax.optimization_barrier((moved_a, layer_out))
    mine_a, other_a = call(sum_kernel, pair, *moved_a)
    pair = [shape(LANES, moved_b[0].shape[1])] * 2
    mine_b, other_b = call(sum_kernel, pair, *moved_b)
    weight_grads = call_at(
        finish_kernel,
        [shape(LANES, 2 * half)] * 2 + [shape(2 * half, LANES)],
        jnp.reshape(row, (1,)),
        mine_a,
        to_core(other_a),
        mine_b,
        to_core(other_b),
    )
    return (layer_out, input_grad, *weight_grads)


def solution(mesh):
    in_specs = (
        P(("depth", "col"), "row"),
        P("row", "col"),
        P("row", "col"),
        P("col", "row"),
        P(("depth", "col"), "row"),
    )
    out_specs = (
        P(("depth", "col"), "row"),
        P(("depth", "col"), "row"),
        P(("row", "depth"), "col"),
        P(("row", "depth"), "col"),
        P("col", ("row", "depth")),
    )
    return jax.shard_map(body, mesh=mesh, in_specs=in_specs, out_specs=out_specs, check_vma=False)
```

```python
import functools

import jax
import jax.numpy as jnp
from jax import lax
from jax.experimental import pallas as pl
from jax.experimental.pallas import tpu as pltpu
from jax.sharding import PartitionSpec as P

BF = jnp.bfloat16
F32 = jnp.float32
COLS, SIDE, LANES = 8, 4, 128
ALONG_X = [[SIDE * y + x for x in range(SIDE)] for y in range(SIDE)]
ALONG_Y = [[SIDE * y + x for y in range(SIDE)] for x in range(SIDE)]
MIB = 1 << 20
CHUNK = 512


def dot(left, right, dims):
    return lax.dot_general(left, right, (dims, ((), ())), preferred_element_type=F32)


def to_z(value, step):
    return lax.ppermute(value, "col", [(k, (k + step) % COLS) for k in range(COLS)])


def to_x(value, step):
    pairs = [(k, k // SIDE * SIDE + (k + step) % SIDE) for k in range(SIDE * SIDE)]
    return lax.ppermute(value, "depth", pairs)


def to_y(value, step):
    side = SIDE * SIDE
    return lax.ppermute(value, "depth", [(k, (k + SIDE * step) % side) for k in range(side)])


def to_core(value):
    return lax.ppermute(value, "row", [(0, 1), (1, 0)])


def swap(value, groups):
    return lax.all_to_all(
        value, "depth", split_axis=0, concat_axis=0, axis_index_groups=groups, tiled=True
    )


def shape(*dims, dtype=BF):
    return jax.ShapeDtypeStruct(dims, dtype)


def hbm(*values):
    return [pltpu.with_memory_space_constraint(value, pltpu.HBM) for value in values]


def cost(flops, moved):
    return pl.CostEstimate(flops=flops, bytes_accessed=moved, transcendentals=0)


def call(kernel, outs, *args, limit=16, scratch=()):
    return pl.pallas_call(
        kernel,
        out_shape=outs,
        scratch_shapes=list(scratch),
        compiler_params=pltpu.CompilerParams(vmem_limit_bytes=limit * MIB),
    )(*args)


def assemble(blocks, feat, upst, send_a, send_b, feat32, upst32):
    rows = blocks[0].shape[0] // 2
    width = feat.shape[1]
    for k in range(COLS):
        if k < COLS // 2:
            block = blocks[k][...].astype(F32)
        elif k == COLS // 2:
            block = jnp.concatenate([blocks[k][...], blocks[k + 1][...]], axis=1).astype(F32)
        else:
            block = blocks[k + 1][...].astype(F32)
        feat32[pl.ds(rows * k, rows), :] = block[:rows]
        upst32[pl.ds(rows * k, rows), :] = block[rows:]
    feat[...] = feat32[...].astype(BF)
    upst[...] = upst32[...].astype(BF)
    quarter = width // SIDE
    for i in range(SIDE):
        send_b[i] = feat[:, quarter * i : quarter * (i + 1)]
        for j in range(SIDE):
            column = LANES * (SIDE * j + i)
            send_a[i, :, LANES * j : LANES * (j + 1)] = feat[:, column : column + LANES]
            send_a[i, :, quarter + LANES * j : quarter + LANES * (j + 1)] = upst[
                :, column : column + LANES
            ]


def gather_col(value):
    half = value.shape[1] // 2
    before, after = to_z(value, 1), to_z(value, -1)
    before2, after2 = to_z(value, 2), to_z(value, -2)
    before3, after3 = to_z(before2, 1), to_z(after2, -1)
    far = (to_z(before2[:, :half], 2), to_z(after2[:, half:], -2))
    return [value, after, after2, after3, *far, before3, before2, before]


def started(moves, sems):
    copies = [pltpu.make_async_copy(*move, sems.at[k]) for k, move in enumerate(moves)]
    for copy in copies:
        copy.start()
    return copies


def weight_copies(which, weights, targets, sems):
    model, half = targets[0].shape
    own = pl.ds(pl.multiple_of(which[0] * half, LANES), half)

    def pair(k):
        at = pl.ds(pl.multiple_of(CHUNK * k, CHUNK), CHUNK)
        return [
            pltpu.make_async_copy(weights[j].at[at, own], targets[j].at[at], sems.at[2 * k + j])
            for j in range(2)
        ]

    last = pltpu.make_async_copy(weights[2].at[own], targets[2], sems.at[2 * model // CHUNK])
    for k in range(model // CHUNK):
        for copy in pair(k):
            copy.start()
    last.start()
    return pair, last


def products(copies, feat, upst, weights, out):
    model, half = weights[0].shape
    pair, last = copies
    out[:, : 2 * half] = jnp.zeros((out.shape[0], 2 * half), F32)

    def step(k, carry):
        at = pl.ds(pl.multiple_of(CHUNK * k, CHUNK), CHUNK)
        for j, copy in enumerate(pair(k)):
            copy.wait()
            place = slice(half * j, half * (j + 1))
            out[:, place] += dot(feat[:, at], weights[j][at, :], ((1,), (0,)))
        return carry

    lax.fori_loop(0, model // CHUNK, step, 0)
    last.wait()
    out[:, 2 * half :] = dot(upst[...], weights[2][...], ((1,), (1,)))


def first_kernel(which, *refs):
    blocks, weights, outs = refs[: COLS + 1], refs[COLS + 1 : COLS + 4], refs[COLS + 4 : COLS + 9]
    out, *assembled = outs
    *targets, feat32, upst32, sems = refs[COLS + 9 :]
    copies = weight_copies(which, weights, targets, sems)
    assemble(blocks, *assembled, feat32, upst32)
    products(copies, *assembled[:2], targets, out)


def second_kernel(which, feat, upst, gate, up, down, out, *scratch):
    targets, sems = scratch[:3], scratch[3]
    copies = weight_copies(which, (gate, up, down), targets, sems)
    products(copies, feat, upst, targets, out)


def in_hbm(kernel, outs, which, vmem, operands, scratch, copies, work, limit):
    return pl.pallas_call(
        kernel,
        in_specs=[pl.BlockSpec(memory_space=pltpu.SMEM)]
        + [pl.BlockSpec(memory_space=pltpu.VMEM)] * len(vmem)
        + [pl.BlockSpec(memory_space=pl.ANY)] * len(operands),
        out_specs=jax.tree.map(
            lambda out: (
                pl.BlockSpec(memory_space=pltpu.VMEM)
                if isinstance(out, jax.ShapeDtypeStruct)
                else pl.BlockSpec()
            ),
            outs,
        ),
        out_shape=outs,
        scratch_shapes=[pltpu.VMEM(*s) for s in scratch] + [pltpu.SemaphoreType.DMA((copies,))],
        cost_estimate=cost(*work),
        compiler_params=pltpu.CompilerParams(vmem_limit_bytes=limit * MIB),
    )(which, *vmem, *hbm(*operands))


def project(which, arrays, weights, rows=None):
    model, units = weights[0].shape
    half = units // 2
    group = COLS * rows if rows else arrays[0].shape[0]
    outs = [shape(group, 3 * half, dtype=F32)]
    scratch = [((model, half), BF)] * 2 + [((half, model), BF)]
    if rows:
        width = SIDE * LANES
        outs += [shape(group, model)] * 2
        outs += [pltpu.HBM((SIDE, group, n), BF) for n in (2 * width, width)]
        scratch += [((group, model), F32)] * 2
    return in_hbm(
        first_kernel if rows else second_kernel,
        outs,
        jnp.reshape(which, (1,)),
        arrays,
        weights,
        scratch,
        2 * model // CHUNK + 1,
        (0, 0),
        28,
    )


def swiglu_kernel(own, theirs, route_a, route_b, grads):
    half = own.shape[1] // 3
    cut = route_a.shape[1] - half
    parts = [slice(half * k, half * (k + 1)) for k in range(3)]
    gate_pre = own[:, parts[0]] + theirs[:, parts[0]]
    up_pre = own[:, parts[1]] + theirs[:, parts[1]]
    hidden_grad = own[:, parts[2]] + theirs[:, parts[2]]
    logistic = jax.nn.sigmoid(gate_pre)
    hidden = (gate_pre * logistic * up_pre).astype(BF)
    gate_grad = hidden_grad * up_pre * logistic * (1.0 + gate_pre * (1.0 - logistic))
    gate_grad = gate_grad.astype(BF)
    up_grad = (hidden_grad * gate_pre * logistic).astype(BF)
    route_a[:, :half] = hidden
    route_a[:, half:] = gate_grad[:, :cut]
    route_b[:, : half - cut] = gate_grad[:, cut:]
    route_b[:, half - cut :] = up_grad
    for part, value in zip(parts, (gate_grad, up_grad, hidden)):
        grads[:, part] = value


def whole_moves(place, half, own, theirs, parts, targets):
    moves = []
    for part, target in zip(parts, targets):
        for source, which in ((own, place[0]), (theirs, 1 - place[0])):
            at = pl.ds(pl.multiple_of(which * half, LANES), half)
            moves.append((source.at[:, pl.ds(half * part, half)], target.at[:, at]))
    return moves


def store_blocks(place, out, total, base):
    rows, width = out.shape[1], total.shape[1]
    for k in range(COLS):
        at = lax.rem(place[1] + k, COLS)
        out[at, :, base : base + width] = total[pl.ds(rows * k, rows), :].astype(BF)


def forward_kernel(place, theirs, own, down, out, hidden, down_v, total, sems):
    units = down.shape[0]
    size = CHUNK // 2
    moves = whole_moves(place, units // 2, own, theirs, (2,), (hidden,))
    copies = started(moves, sems)

    def part(k):
        at = pl.ds(pl.multiple_of(size * k, size), size)
        return pltpu.make_async_copy(down.at[at], down_v.at[at], sems.at[2 + k])

    for k in range(units // size):
        part(k).start()
    total[...] = jnp.zeros(total.shape, F32)
    for copy in copies:
        copy.wait()

    def step(k, carry):
        part(k).wait()
        at = pl.ds(pl.multiple_of(size * k, size), size)
        total[...] += dot(hidden[:, at], down_v[at, :], ((1,), (0,)))
        return carry

    lax.fori_loop(0, units // size, step, 0)
    store_blocks(place, out, total, 0)


def backward_kernel(
    place, first, theirs, own, gate, up, out, gate_g, up_g, gate_v, up_v, total, sems
):
    model, units = gate.shape
    moves = whole_moves(place, units // 2, own, theirs, (0, 1), (gate_g, up_g))
    moves.append((first, out.at[:, :, pl.ds(0, model)]))
    copies = started(moves, sems)

    def pair(k):
        at = pl.ds(pl.multiple_of(CHUNK * k, CHUNK), CHUNK)
        return [
            pltpu.make_async_copy(source.at[at], target.at[at], sems.at[5 + 2 * k + j])
            for j, (source, target) in enumerate(((gate, gate_v), (up, up_v)))
        ]

    for k in range(model // CHUNK):
        for copy in pair(k):
            copy.start()
    for copy in copies:
        copy.wait()

    def step(k, carry):
        for copy in pair(k):
            copy.wait()
        at = pl.ds(pl.multiple_of(CHUNK * k, CHUNK), CHUNK)
        product = dot(gate_g[...], gate_v[at, :], ((1,), (1,)))
        total[:, at] = product + dot(up_g[...], up_v[at, :], ((1,), (1,)))
        return carry

    lax.fori_loop(0, model // CHUNK, step, 0)
    store_blocks(place, out, total, model)


def forward(place, grads, down_weight, rows):
    units, model = down_weight.shape
    group = COLS * rows
    return in_hbm(
        forward_kernel,
        shape(COLS, rows, model),
        place,
        grads[1:],
        (grads[0], down_weight),
        [((group, units), BF), ((units, model), BF), ((group, model), F32)],
        2 + 2 * units // CHUNK,
        (2 * group * model * units, 2 * model * units),
        16,
    )


def backward(place, grads, gate_weight, up_weight, first, rows):
    model, units = gate_weight.shape
    group = COLS * rows
    return in_hbm(
        backward_kernel,
        shape(COLS, rows, 2 * model),
        place,
        (first, grads[1]),
        (grads[0], gate_weight, up_weight),
        [((group, units), BF)] * 2 + [((model, units), BF)] * 2 + [((group, model), F32)],
        5 + 2 * model // CHUNK,
        (4 * group * model * units, 4 * model * units),
        28,
    )


def weight_kernel(cut, place, *refs):
    pieces = (*refs[1:4], refs[0])
    own, before, after, far_a, far_b, piece, columns, sems = refs[6:]
    group, wide = pieces[0].shape
    width = SIDE * LANES
    around = (0, SIDE - 1, 1, 2)
    moves = [(pieces[s], piece.at[pl.ds(group * s, group)]) for s in range(SIDE)]
    moves += [(refs[4 + t], columns.at[t]) for t in range(2)]
    sources = [lax.rem(place[0] + offset, SIDE) for offset in around]
    for copy in started(moves, sems):
        copy.wait()
    for ref, offset in ((far_a, 2), (after, 1), (before, SIDE - 1), (own, 0)):
        start = LANES * lax.rem(place[1] + offset, SIDE)
        for first, last, base in ((0, cut, width), (cut, wide, 0)):
            if first == last:
                continue
            at = pl.ds(pl.multiple_of(base + start, LANES), LANES)
            left = jnp.concatenate(
                [
                    jnp.concatenate([columns[t, source, :, at] for t in range(2)], axis=1)
                    for source in sources
                ],
                axis=0,
            )
            value = dot(left, piece[:, first:last], ((0,), (0,)))
            if ref is far_a:
                far_a[:, first:last] = value[:LANES].astype(BF)
                far_b[:, first:last] = value[LANES:].astype(BF)
            else:
                ref[:, first:last] = value.astype(ref.dtype)


def weight_partials(cut, place, pieces, columns):
    group, wide = pieces[0].shape
    tokens, width = SIDE * group, columns[0].shape[2]
    return in_hbm(
        functools.partial(weight_kernel, cut),
        [shape(2 * LANES, wide, dtype=F32)]
        + [shape(2 * LANES, wide)] * 2
        + [shape(LANES, wide)] * 2,
        place,
        () if cut else pieces[3:],
        (*(pieces[3:] if cut else ()), *pieces[:3], *columns),
        [((tokens, wide), BF), ((2, *columns[0].shape), BF)],
        SIDE + 2,
        (16 * tokens * LANES * wide, 2 * tokens * (wide + 2 * width)),
        20,
    )


def pass_on_kernel(before, after, from_before, from_after, send_before, send_after):
    first, second = pl.ds(0, LANES), pl.ds(LANES, LANES)
    total = after[first, :].astype(F32) + from_before[...].astype(F32)
    send_after[first, :] = total.astype(BF)
    send_after[second, :] = after[second, :]
    send_before[first, :] = before[first, :]
    total = before[second, :].astype(F32) + from_after[...].astype(F32)
    send_before[second, :] = total.astype(BF)


def sum_kernel(own, from_before, from_after, mine, theirs):
    total = own[...] + from_before[...].astype(F32) + from_after[...].astype(F32)
    mine[...] = total[:LANES].astype(BF)
    theirs[...] = total[LANES:].astype(BF)


def scatter(cut, place, pieces, columns, send):
    wide = pieces[0].shape[1]
    own, before, after, far_a, far_b = weight_partials(cut, place, pieces, columns)
    from_before, from_after = send(far_a, 1), send(far_b, -1)
    pair = [shape(2 * LANES, wide)] * 2
    send_before, send_after = call(pass_on_kernel, pair, before, after, from_before, from_after)
    return own, send(send_after, 1), send(send_before, -1)


def finish_kernel(which, mine_a, other_a, mine_b, other_b, gate, up, down):
    half = gate.shape[1] // 2
    cut = mine_a.shape[1] - half
    rest = half - cut

    def place(a, b, base):
        gate[:, base : base + cut] = a[:, half:]
        gate[:, base + cut : base + half] = b[:, :rest]
        up[:, base : base + half] = b[:, rest:]
        down[base : base + half, :] = a[:, :half].T

    @pl.when(which[0] == 0)
    def _():
        place(mine_a, mine_b, 0)
        place(other_a, other_b, half)

    @pl.when(which[0] != 0)
    def _():
        place(other_a, other_b, 0)
        place(mine_a, mine_b, half)


def total_kernel(moved, out, grad):
    model = out.shape[1]
    total = moved[0].astype(F32)
    for k in range(1, COLS):
        total = total + moved[k].astype(F32)
    out[...] = total[:, :model].astype(BF)
    grad[...] = total[:, model:].astype(BF)


def call_at(kernel, outs, which, *args):
    return pl.pallas_call(
        kernel,
        in_specs=[pl.BlockSpec(memory_space=pltpu.SMEM)]
        + [pl.BlockSpec(memory_space=pltpu.VMEM)] * len(args),
        out_shape=outs,
        compiler_params=pltpu.CompilerParams(vmem_limit_bytes=16 * MIB),
    )(which, *args)


def gather(value, send):
    before, after = send(value, 1), send(value, -1)
    return [value, before, after, send(before, 1)]


def body(tokens, gate_weight, up_weight, down_weight, cotangent):
    row, col, depth = (lax.axis_index(name) for name in ("row", "col", "depth"))
    at_x, at_y = depth % SIDE, depth // SIDE
    rows, model = tokens.shape
    group = rows * COLS
    half = gate_weight.shape[1] // 2
    cut = (half // LANES // 2 + 2) * LANES

    blocks = gather_col(jnp.concatenate([tokens, cotangent], axis=0))
    weights = (gate_weight, up_weight, down_weight)
    sent, features, upstream, send_a, send_b = project(1 - row, blocks, weights, rows)
    (kept,) = project(row, (features, upstream), weights)
    route_a, route_b, grads = call(
        swiglu_kernel,
        [pltpu.HBM((group, n), BF) for n in (half + cut, 2 * half - cut, 3 * half)],
        kept,
        to_core(sent),
    )
    columns_a = swap(send_a, ALONG_X)

    grads = (grads, to_core(grads))
    before_a, after_a = to_x(route_a, 1), to_x(route_a, -1)
    before_b, after_b = to_y(route_b, 1), to_y(route_b, -1)
    place = jnp.stack([row, col])
    first = forward(place, grads, down_weight, rows)
    columns_a, send_b, first = lax.optimization_barrier((columns_a, send_b, first))
    columns_b = swap(send_b, ALONG_Y)
    columns_a = (columns_a, to_core(columns_a))
    columns_b = (columns_b, to_core(columns_b))

    before_a, after_b, first = lax.optimization_barrier((before_a, after_b, first))
    grads, _ = lax.optimization_barrier((grads, (before_a, before_b, after_a, after_b)))
    part = backward(place, grads, gate_weight, up_weight, first, rows)
    wide_a = [route_a, before_a, after_a, to_x(before_a, 1)]
    wide_b = [route_b, before_b, after_b, to_y(after_b, -1)]
    wide_a[1], wide_b[1], part = lax.optimization_barrier((wide_a[1], wide_b[1], part))
    part, _ = lax.optimization_barrier((part, (wide_a[3], wide_b[3])))
    moved = lax.all_to_all(part, "col", split_axis=0, concat_axis=0, tiled=True)
    layer_out, input_grad = call(total_kernel, [shape(rows, model)] * 2, moved)

    moved_a = scatter(half, jnp.stack([at_x, at_y]), wide_a, columns_a, to_y)
    moved_b = scatter(0, jnp.stack([at_y, at_x]), wide_b, columns_b, to_x)
    pair = [shape(LANES, moved_a[0].shape[1])] * 2
    moved_a, layer_out = lax.optimization_barrier((moved_a, layer_out))
    mine_a, other_a = call(sum_kernel, pair, *moved_a)
    pair = [shape(LANES, moved_b[0].shape[1])] * 2
    mine_b, other_b = call(sum_kernel, pair, *moved_b)
    weight_grads = call_at(
        finish_kernel,
        [shape(LANES, 2 * half)] * 2 + [shape(2 * half, LANES)],
        jnp.reshape(row, (1,)),
        mine_a,
        to_core(other_a),
        mine_b,
        to_core(other_b),
    )
    return (layer_out, input_grad, *weight_grads)


def solution(mesh):
    in_specs = (
        P(("depth", "col"), "row"),
        P("row", "col"),
        P("row", "col"),
        P("col", "row"),
        P(("depth", "col"), "row"),
    )
    out_specs = (
        P(("depth", "col"), "row"),
        P(("depth", "col"), "row"),
        P(("row", "depth"), "col"),
        P(("row", "depth"), "col"),
        P("col", ("row", "depth")),
    )
    return jax.shard_map(body, mesh=mesh, in_specs=in_specs, out_specs=out_specs, check_vma=False)
```
